32 devices in a mesh: ctx: 8 (over z, y), head: 4 (over x, core).
Axes of the slice: x: 2, y: 2, z: 4, core: 2. Of those that a mesh axis runs over, the one named last changes fastest.
Arguments:
- queries: bfloat16 [1024, 4096], P('ctx', 'head'), may hold values from -6 to 6
- keys: bfloat16 [1024, 4096], P('ctx', 'head'), may hold values from -0.52734375 to 0.52734375
- values: bfloat16 [1024, 4096], P('ctx', 'head'), may hold values from -6 to 6
- grad_out: bfloat16 [1024, 4096], P('ctx', 'head'), may hold values from -6 to 6
- token_kind: int32 [1024], P('ctx'), may hold values from 0 to 1
- level_table: int32 [2, 32, 8], P(None, 'head'), may hold values from 1 to 8
- head_scale: float32 [32], P('head'), may hold values from 0.5 to 4
- norm_gain: float32 [4096], P('head'), may hold values from 0.5 to 1.5
Outputs:
- attended: bfloat16 [1024, 4096], P('ctx', 'head')
- grad_queries: bfloat16 [1024, 4096], P('ctx', 'head')
- grad_keys: bfloat16 [1024, 4096], P('ctx', 'head')
- grad_values: bfloat16 [1024, 4096], P('ctx', 'head')
The draws below stay inside these ranges and needn't reach their ends.
All inputs are finite; a program needn't handle non-finite values.
Results may differ from the reference program's by a relative error of at most 0.0057.
Values may be sent and summed in bfloat16 or wider, within the bound.
A program may use at most 64 MiB of HBM per device.

```python
import math
import jax
import jax.numpy as jnp
from jax import lax

HEADS = 32
DH = 128
LEVELS = 8
KINDS = 2
TOK_DEV = 128
TOKENS = 1024
N_CTX = 8


def with_ends(result, rng, least, top_value):
    extent = result.shape
    index_at = [jax.random.randint(jax.random.fold_in(rng, axis), (), 0, extent[axis]) for axis in range(len(extent))]
    result = result.at[tuple(index_at)].set(least)
    longest = extent.index(max(extent))
    index_at[longest] = (index_at[longest] + 1) % extent[longest]
    return result.at[tuple(index_at)].set(top_value)


def levels(stream_key, shape, cuts, low, top_value):
    level = 1.0
    for axis_at, blocks in cuts:
        draws = jax.random.uniform(jax.random.fold_in(jax.random.fold_in(stream_key, 6), axis_at), (blocks,), jnp.float32, low / len(cuts), top_value / len(cuts))
        level = level * jnp.repeat(jnp.exp(draws), shape[axis_at] // blocks).reshape((-1,) + (1,) * (len(shape) - 1 - axis_at))
    return level


def normal_values(own_key, shape, scale, reach, cuts=(), kind=jnp.bfloat16):
    level = levels(own_key, shape, cuts, -0.22, 0.18) if cuts else 1.0
    values = jax.random.normal(own_key, shape, jnp.float32) * scale * level
    return jnp.minimum(jnp.maximum(values, -reach), reach).astype(kind)


def setup_inputs(seed: int = 0) -> dict:
    streams_of = jax.random.split(jax.random.key(seed), 9)
    queries = normal_values(streams_of[0], (TOKENS, HEADS * DH), 1.0, 6.0, ((0, 8), (1, 4)))
    keys = normal_values(streams_of[1], (TOKENS, HEADS * DH), 0.0884, 0.52734375, ((0, 8), (1, 4)))
    values = normal_values(streams_of[2], (TOKENS, HEADS * DH), 1.0, 6.0, ((0, 8), (1, 4)))
    grad_out = normal_values(streams_of[3], (TOKENS, HEADS * DH), 1.0, 6.0, ((0, 8), (1, 4)))
    token_kind = with_ends(jax.random.randint(streams_of[4], (TOKENS,), 0, KINDS), jax.random.fold_in(streams_of[4], 1), 0, KINDS - 1).astype(jnp.int32)
    level_table = with_ends(jax.random.randint(streams_of[5], (KINDS, HEADS, LEVELS), 1, 9), jax.random.fold_in(streams_of[5], 1), 1, 8).astype(jnp.int32)
    head_scale = jnp.clip(jnp.exp(math.log(4.0) - 2.0794415 * jax.random.uniform(streams_of[6], (HEADS,), jnp.float32) ** levels(streams_of[6], (HEADS,), ((0, 4),), -0.2, 0.2)), 0.5, 4.0)
    norm_gain = jnp.clip(1.0 + 0.1 * jax.random.normal(streams_of[7], (HEADS * DH,), jnp.float32), 0.5, 1.5)
    return {"queries": queries, "keys": keys, "values": values, "grad_out": grad_out, "token_kind": token_kind, "level_table": level_table, "head_scale": head_scale, "norm_gain": norm_gain}


EPSILON = 1e-06
HIGHEST_PRECISION = lax.Precision.HIGHEST

def level_factors():
    return 0.25 * jnp.exp2(-0.5 * jnp.arange(LEVELS).astype(jnp.float32))

def rounded(value):
    return lax.optimization_barrier(value.astype(jnp.bfloat16)).astype(jnp.float32)

def sibling_sums(stacked, height):
    span = 2 ** height
    groups = stacked.shape[0] // (2 * span)
    folded = stacked.reshape((groups, 2, span) + stacked.shape[1:]).sum(axis=2)
    swapped = folded[:, ::-1]
    spread = jnp.broadcast_to(swapped[:, :, None], (groups, 2, span) + stacked.shape[1:])
    return spread.reshape(stacked.shape)

def upper_flags(block_total, height):
    return (jnp.arange(block_total) // 2 ** height % 2).astype(jnp.float32)

def einsum_high(form, left, right):
    return jnp.einsum(form, left, right, precision=HIGHEST_PRECISION)

def block_states(key_f, value_f):
    return einsum_high('nsd,nse->nde', key_f, value_f)

def block_probs(query_f, key_f, level_weights):
    causal = jnp.tril(jnp.ones((TOK_DEV, TOK_DEV), dtype=bool))
    scores = einsum_high('nsd,nud->nsu', query_f, key_f)
    return rounded(jnp.where(causal[None], scores, 0.0) * level_weights[:, :, 0:1])

def head_forward(operands):
    query_rows, key_rows, value_rows, level_weights = operands
    query_f = query_rows.astype(jnp.float32)
    key_f = key_rows.astype(jnp.float32)
    value_f = value_rows.astype(jnp.float32)
    block_total = N_CTX
    tree_depth = N_CTX.bit_length() - 1
    attn_probs = block_probs(query_f, key_f, level_weights)
    readout = einsum_high('nsu,nud->nsd', attn_probs, value_f)
    states = block_states(key_f, value_f)
    for height in range(tree_depth):
        flags = upper_flags(block_total, height)[:, None, None]
        bucket = rounded(sibling_sums(states, height) * flags)
        readout = readout + level_weights[:, :, height + 1, None] * einsum_high('nsd,nde->nse', query_f, bucket)
    return readout

def head_backward(operands):
    query_rows, key_rows, value_rows, grad_rows, level_weights = operands
    query_f = query_rows.astype(jnp.float32)
    key_f = key_rows.astype(jnp.float32)
    value_f = value_rows.astype(jnp.float32)
    grad_f = grad_rows.astype(jnp.float32)
    block_total = N_CTX
    tree_depth = N_CTX.bit_length() - 1
    causal = jnp.tril(jnp.ones((TOK_DEV, TOK_DEV), dtype=bool))
    attn_probs = block_probs(query_f, key_f, level_weights)
    grad_scores = einsum_high('nse,nue->nsu', grad_f, value_f)
    grad_probs = rounded(jnp.where(causal[None], grad_scores, 0.0) * level_weights[:, :, 0:1])
    grad_query = einsum_high('nsu,nud->nsd', grad_probs, key_f)
    grad_key = einsum_high('nsu,nsd->nud', grad_probs, query_f)
    grad_value = einsum_high('nsu,nse->nue', attn_probs, grad_f)
    states = block_states(key_f, value_f)
    grad_states = jnp.zeros_like(states)
    for height in range(tree_depth):
        flags = upper_flags(block_total, height)[:, None, None]
        bucket = rounded(sibling_sums(states, height) * flags)
        weight_now = level_weights[:, :, height + 1, None]
        grad_query = grad_query + weight_now * einsum_high('nse,nde->nsd', grad_f, bucket)
        weighted = weight_now * grad_f
        grad_part = einsum_high('nsd,nse->nde', query_f, weighted) * flags
        grad_states = grad_states + sibling_sums(grad_part, height)
    state_bf = rounded(grad_states)
    grad_key = grad_key + einsum_high('nse,nde->nsd', value_f, state_bf)
    grad_value = grad_value + einsum_high('nsd,nde->nse', key_f, state_bf)
    return (grad_query.astype(jnp.bfloat16), grad_key.astype(jnp.bfloat16), grad_value.astype(jnp.bfloat16))

def reference(queries, keys, values, grad_out, token_kind, level_table, head_scale, norm_gain):
    block_total = N_CTX
    weight_table = level_table.astype(jnp.float32) * level_factors()[None, None, :]
    token_weights = weight_table[token_kind]

    def by_head(array):
        return array.reshape(block_total, TOK_DEV, HEADS, -1).transpose(2, 0, 1, 3)

    def by_token(array):
        return array.transpose(1, 2, 0, 3).reshape(TOKENS, HEADS * DH)
    head_weights = by_head(token_weights)
    query_heads = by_head(queries)
    key_heads = by_head(keys)
    value_heads = by_head(values)
    readout = lax.map(head_forward, (query_heads, key_heads, value_heads, head_weights))
    scale = head_scale[:, None, None, None]
    gain = norm_gain.reshape(HEADS, 1, 1, DH)
    scaled = readout * scale
    feature_count = HEADS * DH
    square_sum = lax.optimization_barrier(jnp.sum(scaled * scaled, axis=(0, 3)))[None, :, :, None]
    rms_value = jnp.sqrt(square_sum / feature_count + EPSILON)
    attended = (scaled / rms_value * gain).astype(jnp.bfloat16)
    upstream = by_head(grad_out).astype(jnp.float32)
    cross_sum = lax.optimization_barrier(jnp.sum(gain * upstream * scaled, axis=(0, 3)))[None, :, :, None]
    grad_scaled = gain * upstream / rms_value - scaled * (cross_sum / (feature_count * rms_value ** 3))
    grad_output = (grad_scaled * scale).astype(jnp.bfloat16)
    grads = lax.map(head_backward, (query_heads, key_heads, value_heads, grad_output, head_weights))
    return (by_token(attended), by_token(grads[0]), by_token(grads[1]), by_token(grads[2]))
```

```python
import functools

import jax
import jax.numpy as jnp
from jax import lax
from jax.experimental import pallas as pl
from jax.experimental.pallas import tpu as pltpu
from jax.sharding import PartitionSpec as P

EPSILON = 1e-06
CHUNK = 2
F32 = jnp.float32
BF16 = jnp.bfloat16


def factor(level):
    return 0.25 * 2.0 ** (-0.5 * level)


def dot(left, right, contract):
    return lax.dot_general(left, right, (contract, ((), ())), preferred_element_type=F32)


NN = ((1,), (0,))
NT = ((1,), (1,))
TN = ((0,), (0,))


def kernel(
    ctx_count, head_count,
    q_hbm, k_hbm, v_hbm, dy_hbm, kind_ref, table_ref, scale_ref, gain_ref,
    att_ref, gq_ref, gk_ref, gv_ref,
    q_ref, k_ref, v_ref, dy_ref, kind_col, inv_col, coef_col,
    states, probs, query_t, readout, grad_out_ref, kind_sums, grad_states, key_acc, value_acc,
    fwd_send, fwd_recv, bwd_send, bwd_recv, stat_send, stat_recv,
    load_sem, fwd_ssem, fwd_rsem, bwd_ssem, bwd_rsem, stat_ssem, stat_rsem,
):
    tokens, width = q_ref.shape
    heads, size, _ = states.shape
    kinds = table_ref.shape[0]
    depth = ctx_count.bit_length() - 1
    chunks = heads // CHUNK
    c = lax.axis_index("ctx")
    me = lax.axis_index("head")
    partner = [c ^ (1 << b) for b in range(depth)]
    bit = [(c >> b) & 1 for b in range(depth)]
    upper = [bit[b] == 1 for b in range(depth)]
    need = [(c >> (b + 1)) != (ctx_count >> (b + 1)) - 1 for b in range(depth)]
    fwd_sends = [jnp.logical_or(bit[b] == 0, need[b]) for b in range(depth)]
    fwd_recvs = [jnp.logical_or(bit[b] == 1, need[b]) for b in range(depth)]
    bwd_sends = fwd_recvs
    bwd_recvs = fwd_sends

    loads = [
        pltpu.make_async_copy(src, dst, load_sem.at[i])
        for i, (src, dst) in enumerate(
            ((k_hbm, k_ref), (v_hbm, v_ref), (q_hbm, q_ref), (dy_hbm, dy_ref))
        )
    ]
    for load in loads:
        load.start()
    barrier = pltpu.get_barrier_semaphore()
    for b in range(depth):
        pl.semaphore_signal(barrier, inc=1, device_id={"ctx": partner[b]}, device_id_type=pl.DeviceIdType.MESH)
    for d in range(1, head_count):
        pl.semaphore_signal(
            barrier, inc=1, device_id={"head": lax.rem(me + d, head_count)},
            device_id_type=pl.DeviceIdType.MESH,
        )

    def cols(h):
        return pl.ds(h * size, size)

    def chunk_heads(j):
        return range(j * CHUNK, (j + 1) * CHUNK)

    def exchange(send, recv, ssem, rsem, b, j):
        part = pl.ds(j * CHUNK, CHUNK)
        return pltpu.make_async_remote_copy(
            src_ref=send.at[b, part], dst_ref=recv.at[b, part],
            send_sem=ssem.at[b, j], recv_sem=rsem.at[b, j],
            device_id={"ctx": partner[b]}, device_id_type=pl.DeviceIdType.MESH,
        )

    fwd = functools.partial(exchange, fwd_send, fwd_recv, fwd_ssem, fwd_rsem)
    bwd = functools.partial(exchange, bwd_send, bwd_recv, bwd_ssem, bwd_rsem)

    def weight(kind, h, level):
        return table_ref[kind, h, level].astype(F32) * factor(level)

    def token_weights(h, level):
        out = jnp.full((tokens, size), weight(0, h, level), F32)
        for kind in range(1, kinds):
            out = jnp.where(kind_col[...] == kind, weight(kind, h, level), out)
        return out

    def causal():
        row = lax.broadcasted_iota(jnp.int32, (tokens, tokens), 0)
        col = lax.broadcasted_iota(jnp.int32, (tokens, tokens), 1)
        return col <= row

    loads[0].wait()
    loads[1].wait()
    for j in range(chunks):
        for h in chunk_heads(j):
            state = dot(k_ref[:, cols(h)], v_ref[:, cols(h)], TN)
            states[h] = state
            fwd_send[0, h] = state.astype(BF16)
        if j == 0:
            pl.semaphore_wait(barrier, depth + head_count - 1)

        @pl.when(fwd_sends[0])
        def _():
            fwd(0, j).start()

    loads[2].wait()
    loads[3].wait()
    kind_col[...] = jnp.transpose(
        jnp.broadcast_to(kind_ref[...].astype(F32), (size, tokens))
    )

    def local_forward(j):
        for h in chunk_heads(j):
            q = q_ref[:, cols(h)]
            scores = dot(q, k_ref[:, cols(h)], NT)
            attn = (jnp.where(causal(), scores, 0.0) * token_weights(h, 0)).astype(BF16)
            probs[h] = attn
            readout[h] = dot(attn, v_ref[:, cols(h)], NN)
            query_t[h] = jnp.transpose(q)

    def receive_forward(b, j):
        @pl.when(fwd_recvs[b])
        def _():
            fwd(b, j).wait_recv()
            if b + 1 < depth:
                for h in chunk_heads(j):
                    total = states[h] + fwd_recv[b, h].astype(F32)
                    states[h] = total
                    fwd_send[b + 1, h] = total.astype(BF16)

        if b + 1 < depth:

            @pl.when(fwd_sends[b + 1])
            def _():
                fwd(b + 1, j).start()

        @pl.when(upper[b])
        def _():
            for h in chunk_heads(j):
                level = dot(q_ref[:, cols(h)], fwd_recv[b, h], NN)
                readout[h] += token_weights(h, b + 1) * level

    squares = jnp.zeros((tokens, size), F32)
    crosses = jnp.zeros((tokens, size), F32)
    for step in range(chunks + depth - 1):
        if step < chunks:
            local_forward(step)
        for b in reversed(range(depth)):
            j = step - b
            if 0 <= j < chunks:
                receive_forward(b, j)
        j = step - depth + 1
        if 0 <= j < chunks:
            for h in chunk_heads(j):
                z = readout[h] * scale_ref[h]
                readout[h] = z
                squares += z * z
                crosses += gain_ref[:, cols(h)] * dy_ref[:, cols(h)].astype(F32) * z

    stat_send[0:1, :] = jnp.sum(jnp.transpose(squares), axis=0, keepdims=True)
    stat_send[1:2, :] = jnp.sum(jnp.transpose(crosses), axis=0, keepdims=True)
    stat_copies = [
        pltpu.make_async_remote_copy(
            src_ref=stat_send, dst_ref=stat_recv.at[d - 1],
            send_sem=stat_ssem.at[d - 1], recv_sem=stat_rsem.at[d - 1],
            device_id={"head": lax.rem(me + d, head_count)},
            device_id_type=pl.DeviceIdType.MESH,
        )
        for d in range(1, head_count)
    ]
    for copy in stat_copies:
        copy.start()
    square_row = stat_send[0:1, :]
    cross_row = stat_send[1:2, :]
    for d, copy in enumerate(stat_copies):
        copy.wait_recv()
        square_row += stat_recv[d, 0:1, :]
        cross_row += stat_recv[d, 1:2, :]
    features = width * head_count
    rms = jnp.sqrt(square_row / features + EPSILON)
    coef = cross_row / (features * rms * rms * rms)
    inv_col[...] = jnp.transpose(jnp.broadcast_to(1.0 / rms, (size, tokens)))
    coef_col[...] = jnp.transpose(jnp.broadcast_to(coef, (size, tokens)))

    def message(b, h, flag):
        total = None
        for kind in range(kinds):
            term = (weight(kind, h, b + 1) * flag) * kind_sums[h, :, pl.ds(kind * size, size)]
            total = term if total is None else total + term
        return total

    for j in range(chunks):
        for h in chunk_heads(j):
            gain = gain_ref[:, cols(h)]
            z = readout[h]
            att_ref[:, cols(h)] = (z * inv_col[...] * gain).astype(BF16)
            grad = gain * dy_ref[:, cols(h)].astype(F32) * inv_col[...] - z * coef_col[...]
            grad = (grad * scale_ref[h]).astype(BF16)
            grad_out_ref[h] = grad
            masked = jnp.concatenate(
                [jnp.where(kind_col[...] == kind, grad.astype(F32), 0.0).astype(BF16) for kind in range(kinds)],
                axis=1,
            )
            kind_sums[h] = dot(query_t[h], masked, NN)
            grad_states[h] = jnp.zeros((size, size), F32)

        @pl.when(bwd_sends[depth - 1])
        def _():
            for h in chunk_heads(j):
                bwd_send[depth - 1, h] = message(depth - 1, h, 1.0).astype(BF16)
            bwd(depth - 1, j).start()

    def local_backward(j):
        for h in chunk_heads(j):
            grad = grad_out_ref[h]
            scores = dot(grad, v_ref[:, cols(h)], NT)
            dprobs = (jnp.where(causal(), scores, 0.0) * token_weights(h, 0)).astype(BF16)
            key_acc[h] = dot(dprobs, q_ref[:, cols(h)], TN)
            value_acc[h] = dot(probs[h], grad, TN)
            readout[h] = dot(dprobs, k_ref[:, cols(h)], NN)
        for b in range(depth):

            @pl.when(upper[b])
            def _():
                for h in chunk_heads(j):
                    level = dot(grad_out_ref[h], fwd_recv[b, h], NT)
                    readout[h] += token_weights(h, b + 1) * level

        for h in chunk_heads(j):
            gq_ref[:, cols(h)] = readout[h].astype(BF16)

    def receive_backward(b, j):
        @pl.when(bwd_recvs[b])
        def _():
            bwd(b, j).wait_recv()
            for h in chunk_heads(j):
                grad_states[h] += bwd_recv[b, h].astype(F32)

        if b > 0:

            @pl.when(bwd_sends[b - 1])
            def _():
                flag = bit[b - 1].astype(F32)
                for h in chunk_heads(j):
                    bwd_send[b - 1, h] = (grad_states[h] + message(b - 1, h, flag)).astype(BF16)
                bwd(b - 1, j).start()

        else:
            for h in chunk_heads(j):
                state = grad_states[h].astype(BF16)
                gk_ref[:, cols(h)] = (key_acc[h] + dot(v_ref[:, cols(h)], state, NT)).astype(BF16)
                gv_ref[:, cols(h)] = (value_acc[h] + dot(k_ref[:, cols(h)], state, NN)).astype(BF16)

    for step in range(chunks + depth - 1):
        if step < chunks:
            local_backward(step)
        for b in range(depth):
            j = step - (depth - 1 - b)
            if 0 <= j < chunks:
                receive_backward(b, j)

    for copy in stat_copies:
        copy.wait_send()
    for b in range(depth):

        @pl.when(fwd_sends[b])
        def _():
            for j in range(chunks):
                fwd(b, j).wait_send()

        @pl.when(bwd_sends[b])
        def _():
            for j in range(chunks):
                bwd(b, j).wait_send()


def solution(mesh):
    ctx_count, head_count = mesh.shape["ctx"], mesh.shape["head"]
    depth = ctx_count.bit_length() - 1

    def shards(queries, keys, values, grad_out, token_kind, level_table, head_scale, norm_gain):
        tokens, width = queries.shape
        kinds, heads, _ = level_table.shape
        size = width // heads
        chunks = heads // CHUNK
        anywhere = pl.BlockSpec(memory_space=pl.ANY)
        vmem = pl.BlockSpec(memory_space=pltpu.VMEM)
        smem = pl.BlockSpec(memory_space=pltpu.SMEM)
        block = jax.ShapeDtypeStruct((tokens, width), BF16)
        square = (heads, size, size)
        return pl.pallas_call(
            functools.partial(kernel, ctx_count, head_count),
            out_shape=(block,) * 4,
            in_specs=[anywhere] * 4 + [vmem, smem, smem, vmem],
            out_specs=(vmem,) * 4,
            scratch_shapes=[pltpu.VMEM((tokens, width), BF16)] * 4
            + [pltpu.VMEM((tokens, size), F32)] * 3
            + [
                pltpu.VMEM(square, F32),
                pltpu.VMEM((heads, tokens, tokens), BF16),
                pltpu.VMEM((heads, size, tokens), BF16),
                pltpu.VMEM((heads, tokens, size), F32),
                pltpu.VMEM((heads, tokens, size), BF16),
                pltpu.VMEM((heads, size, kinds * size), F32),
                pltpu.VMEM(square, F32),
                pltpu.VMEM((heads, tokens, size), F32),
                pltpu.VMEM((heads, tokens, size), F32),
            ]
            + [pltpu.VMEM((depth,) + square, BF16)] * 4
            + [
                pltpu.VMEM((8, tokens), F32),
                pltpu.VMEM((head_count - 1, 8, tokens), F32),
                pltpu.SemaphoreType.DMA((4,)),
            ]
            + [pltpu.SemaphoreType.DMA((depth, chunks))] * 4
            + [pltpu.SemaphoreType.DMA((head_count - 1,))] * 2,
            compiler_params=pltpu.CompilerParams(
                collective_id=0, has_side_effects=True, vmem_limit_bytes=40 * 1024 * 1024
            ),
            cost_estimate=pl.CostEstimate(
                flops=36 * heads * tokens * size * size, bytes_accessed=16 * tokens * width, transcendentals=0
            ),
        )(
            queries, keys, values, grad_out,
            token_kind.reshape(1, tokens), level_table, head_scale, norm_gain.reshape(1, width),
        )

    in_specs = (
        P("ctx", "head"),
        P("ctx", "head"),
        P("ctx", "head"),
        P("ctx", "head"),
        P("ctx"),
        P(None, "head", None),
        P("head"),
        P("head"),
    )
    return jax.shard_map(
        shards, mesh=mesh, in_specs=in_specs, out_specs=(P("ctx", "head"),) * 4, check_vma=False
    )
```

```python
import functools

import jax
import jax.numpy as jnp
from jax import lax
from jax.experimental import pallas as pl
from jax.experimental.pallas import tpu as pltpu
from jax.sharding import PartitionSpec as P

EPSILON = 1e-06
CHUNK = 2
F32 = jnp.float32
BF16 = jnp.bfloat16


def factor(level):
    return 0.25 * 2.0 ** (-0.5 * level)


def dot(left, right, contract):
    return lax.dot_general(left, right, (contract, ((), ())), preferred_element_type=F32)


NN = ((1,), (0,))
NT = ((1,), (1,))
TN = ((0,), (0,))


def kernel(
    ctx_count, head_count,
    q_hbm, k_hbm, v_hbm, dy_hbm, kind_hbm, table_hbm, scale_hbm, gain_hbm,
    att_ref, gq_ref, gk_ref, gv_ref,
    q_ref, k_ref, v_ref, dy_ref, kind_ref, table_ref, scale_ref, gain_ref, kind_col, inv_col, coef_col,
    states, probs, query_t, readout, grad_out_ref, kind_sums, grad_states, key_acc, value_acc,
    fwd_send, fwd_recv, bwd_send, bwd_recv, stat_send, stat_recv,
    load_sem, fwd_ssem, fwd_rsem, bwd_ssem, bwd_rsem, stat_ssem, stat_rsem,
):
    tokens, width = q_ref.shape
    heads, size, _ = states.shape
    kinds = table_ref.shape[0]
    depth = ctx_count.bit_length() - 1
    chunks = heads // CHUNK
    c = lax.axis_index("ctx")
    me = lax.axis_index("head")
    partner = [c ^ (1 << b) for b in range(depth)]
    bit = [(c >> b) & 1 for b in range(depth)]
    upper = [bit[b] == 1 for b in range(depth)]
    need = [(c >> (b + 1)) != (ctx_count >> (b + 1)) - 1 for b in range(depth)]
    fwd_sends = [jnp.logical_or(bit[b] == 0, need[b]) for b in range(depth)]
    fwd_recvs = [jnp.logical_or(bit[b] == 1, need[b]) for b in range(depth)]
    bwd_sends = fwd_recvs
    bwd_recvs = fwd_sends

    loads = [
        pltpu.make_async_copy(src, dst, load_sem.at[i])
        for i, (src, dst) in enumerate(
            (
                (k_hbm, k_ref), (v_hbm, v_ref), (q_hbm, q_ref), (dy_hbm, dy_ref),
                (kind_hbm, kind_ref), (table_hbm, table_ref), (scale_hbm, scale_ref), (gain_hbm, gain_ref),
            )
        )
    ]
    for load in loads:
        load.start()
    barrier = pltpu.get_barrier_semaphore()
    for b in range(depth):
        pl.semaphore_signal(barrier, inc=1, device_id={"ctx": partner[b]}, device_id_type=pl.DeviceIdType.MESH)
    for d in range(1, head_count):
        pl.semaphore_signal(
            barrier, inc=1, device_id={"head": lax.rem(me + d, head_count)},
            device_id_type=pl.DeviceIdType.MESH,
        )

    def cols(h):
        return pl.ds(h * size, size)

    def chunk_heads(j):
        return range(j * CHUNK, (j + 1) * CHUNK)

    def exchange(send, recv, ssem, rsem, b, j):
        part = pl.ds(j * CHUNK, CHUNK)
        return pltpu.make_async_remote_copy(
            src_ref=send.at[b, part], dst_ref=recv.at[b, part],
            send_sem=ssem.at[b, j], recv_sem=rsem.at[b, j],
            device_id={"ctx": partner[b]}, device_id_type=pl.DeviceIdType.MESH,
        )

    fwd = functools.partial(exchange, fwd_send, fwd_recv, fwd_ssem, fwd_rsem)
    bwd = functools.partial(exchange, bwd_send, bwd_recv, bwd_ssem, bwd_rsem)

    def weight(kind, h, level):
        return table_ref[kind, h, level].astype(F32) * factor(level)

    def token_weights(h, level):
        out = jnp.full((tokens, size), weight(0, h, level), F32)
        for kind in range(1, kinds):
            out = jnp.where(kind_col[...] == kind, weight(kind, h, level), out)
        return out

    def causal():
        row = lax.broadcasted_iota(jnp.int32, (tokens, tokens), 0)
        col = lax.broadcasted_iota(jnp.int32, (tokens, tokens), 1)
        return col <= row

    loads[0].wait()
    loads[1].wait()
    for j in range(chunks):
        for h in chunk_heads(j):
            state = dot(k_ref[:, cols(h)], v_ref[:, cols(h)], TN)
            states[h] = state
            fwd_send[0, h] = state.astype(BF16)
        if j == 0:
            pl.semaphore_wait(barrier, depth + head_count - 1)

        @pl.when(fwd_sends[0])
        def _():
            fwd(0, j).start()

    for load in loads[2:]:
        load.wait()
    kind_col[...] = jnp.transpose(
        jnp.broadcast_to(kind_ref[...].astype(F32), (size, tokens))
    )

    def local_forward(j):
        for h in chunk_heads(j):
            q = q_ref[:, cols(h)]
            scores = dot(q, k_ref[:, cols(h)], NT)
            attn = (jnp.where(causal(), scores, 0.0) * token_weights(h, 0)).astype(BF16)
            probs[h] = attn
            readout[h] = dot(attn, v_ref[:, cols(h)], NN)
            query_t[h] = jnp.transpose(q)

    def receive_forward(b, j):
        @pl.when(fwd_recvs[b])
        def _():
            fwd(b, j).wait_recv()
            if b + 1 < depth:
                for h in chunk_heads(j):
                    total = states[h] + fwd_recv[b, h].astype(F32)
                    states[h] = total
                    fwd_send[b + 1, h] = total.astype(BF16)

        if b + 1 < depth:

            @pl.when(fwd_sends[b + 1])
            def _():
                fwd(b + 1, j).start()

        @pl.when(upper[b])
        def _():
            for h in chunk_heads(j):
                level = dot(q_ref[:, cols(h)], fwd_recv[b, h], NN)
                readout[h] += token_weights(h, b + 1) * level

    squares = jnp.zeros((tokens, size), F32)
    crosses = jnp.zeros((tokens, size), F32)
    for step in range(chunks + depth - 1):
        if step < chunks:
            local_forward(step)
        for b in range(depth):
            j = step - b
            if 0 <= j < chunks:
                receive_forward(b, j)
        j = step - depth + 1
        if 0 <= j < chunks:
            for h in chunk_heads(j):
                z = readout[h] * scale_ref[h]
                readout[h] = z
                squares += z * z
                crosses += gain_ref[:, cols(h)] * dy_ref[:, cols(h)].astype(F32) * z

    stat_send[0:1, :] = jnp.sum(jnp.transpose(squares), axis=0, keepdims=True)
    stat_send[1:2, :] = jnp.sum(jnp.transpose(crosses), axis=0, keepdims=True)
    stat_copies = [
        pltpu.make_async_remote_copy(
            src_ref=stat_send, dst_ref=stat_recv.at[d - 1],
            send_sem=stat_ssem.at[d - 1], recv_sem=stat_rsem.at[d - 1],
            device_id={"head": lax.rem(me + d, head_count)},
            device_id_type=pl.DeviceIdType.MESH,
        )
        for d in range(1, head_count)
    ]
    for copy in stat_copies:
        copy.start()
    square_row = stat_send[0:1, :]
    cross_row = stat_send[1:2, :]
    for d, copy in enumerate(stat_copies):
        copy.wait_recv()
        square_row += stat_recv[d, 0:1, :]
        cross_row += stat_recv[d, 1:2, :]
    features = width * head_count
    rms = jnp.sqrt(square_row / features + EPSILON)
    coef = cross_row / (features * rms * rms * rms)
    inv_col[...] = jnp.transpose(jnp.broadcast_to(1.0 / rms, (size, tokens)))
    coef_col[...] = jnp.transpose(jnp.broadcast_to(coef, (size, tokens)))

    def message(b, h, flag):
        total = None
        for kind in range(kinds):
            term = (weight(kind, h, b + 1) * flag) * kind_sums[h, :, pl.ds(kind * size, size)]
            total = term if total is None else total + term
        return total

    for j in range(chunks):
        for h in chunk_heads(j):
            gain = gain_ref[:, cols(h)]
            z = readout[h]
            att_ref[:, cols(h)] = (z * inv_col[...] * gain).astype(BF16)
            grad = gain * dy_ref[:, cols(h)].astype(F32) * inv_col[...] - z * coef_col[...]
            grad = (grad * scale_ref[h]).astype(BF16)
            grad_out_ref[h] = grad
            masked = jnp.concatenate(
                [jnp.where(kind_col[...] == kind, grad.astype(F32), 0.0).astype(BF16) for kind in range(kinds)],
                axis=1,
            )
            kind_sums[h] = dot(query_t[h], masked, NN)
            grad_states[h] = jnp.zeros((size, size), F32)

        @pl.when(bwd_sends[depth - 1])
        def _():
            for h in chunk_heads(j):
                bwd_send[depth - 1, h] = message(depth - 1, h, 1.0).astype(BF16)
            bwd(depth - 1, j).start()

    def local_backward(j):
        for h in chunk_heads(j):
            grad = grad_out_ref[h]
            scores = dot(grad, v_ref[:, cols(h)], NT)
            dprobs = (jnp.where(causal(), scores, 0.0) * token_weights(h, 0)).astype(BF16)
            key_acc[h] = dot(dprobs, q_ref[:, cols(h)], TN)
            value_acc[h] = dot(probs[h], grad, TN)
            readout[h] = dot(dprobs, k_ref[:, cols(h)], NN)
        for b in range(depth):

            @pl.when(upper[b])
            def _():
                for h in chunk_heads(j):
                    level = dot(grad_out_ref[h], fwd_recv[b, h], NT)
                    readout[h] += token_weights(h, b + 1) * level

        for h in chunk_heads(j):
            gq_ref[:, cols(h)] = readout[h].astype(BF16)

    def receive_backward(b, j):
        @pl.when(bwd_recvs[b])
        def _():
            bwd(b, j).wait_recv()
            for h in chunk_heads(j):
                grad_states[h] += bwd_recv[b, h].astype(F32)

        if b > 0:

            @pl.when(bwd_sends[b - 1])
            def _():
                flag = bit[b - 1].astype(F32)
                for h in chunk_heads(j):
                    bwd_send[b - 1, h] = (grad_states[h] + message(b - 1, h, flag)).astype(BF16)
                bwd(b - 1, j).start()

        else:
            for h in chunk_heads(j):
                state = grad_states[h].astype(BF16)
                gk_ref[:, cols(h)] = (key_acc[h] + dot(v_ref[:, cols(h)], state, NT)).astype(BF16)
                gv_ref[:, cols(h)] = (value_acc[h] + dot(k_ref[:, cols(h)], state, NN)).astype(BF16)

    for step in range(chunks + depth - 1):
        if step < chunks:
            local_backward(step)
        for b in reversed(range(depth)):
            j = step - (depth - 1 - b)
            if 0 <= j < chunks:
                receive_backward(b, j)

    for copy in stat_copies:
        copy.wait_send()
    for b in range(depth):

        @pl.when(fwd_sends[b])
        def _():
            for j in range(chunks):
                fwd(b, j).wait_send()

        @pl.when(bwd_sends[b])
        def _():
            for j in range(chunks):
                bwd(b, j).wait_send()


def solution(mesh):
    ctx_count, head_count = mesh.shape["ctx"], mesh.shape["head"]
    depth = ctx_count.bit_length() - 1

    def shards(queries, keys, values, grad_out, token_kind, level_table, head_scale, norm_gain):
        tokens, width = queries.shape
        kinds, heads, _ = level_table.shape
        size = width // heads
        chunks = heads // CHUNK
        hbm = pl.BlockSpec(memory_space=pltpu.HBM)
        vmem = pl.BlockSpec(memory_space=pltpu.VMEM)
        block = jax.ShapeDtypeStruct((tokens, width), BF16)
        square = (heads, size, size)
        return pl.pallas_call(
            functools.partial(kernel, ctx_count, head_count),
            out_shape=(block,) * 4,
            in_specs=[hbm] * 8,
            out_specs=(vmem,) * 4,
            scratch_shapes=[pltpu.VMEM((tokens, width), BF16)] * 4
            + [
                pltpu.VMEM((1, tokens), jnp.int32),
                pltpu.SMEM(level_table.shape, jnp.int32),
                pltpu.SMEM((heads,), F32),
                pltpu.VMEM((1, width), F32),
            ]
            + [pltpu.VMEM((tokens, size), F32)] * 3
            + [
                pltpu.VMEM(square, F32),
                pltpu.VMEM((heads, tokens, tokens), BF16),
                pltpu.VMEM((heads, size, tokens), BF16),
                pltpu.VMEM((heads, tokens, size), F32),
                pltpu.VMEM((heads, tokens, size), BF16),
                pltpu.VMEM((heads, size, kinds * size), F32),
                pltpu.VMEM(square, F32),
                pltpu.VMEM((heads, tokens, size), F32),
                pltpu.VMEM((heads, tokens, size), F32),
            ]
            + [pltpu.VMEM((depth,) + square, BF16)] * 4
            + [
                pltpu.VMEM((8, tokens), F32),
                pltpu.VMEM((head_count - 1, 8, tokens), F32),
                pltpu.SemaphoreType.DMA((8,)),
            ]
            + [pltpu.SemaphoreType.DMA((depth, chunks))] * 4
            + [pltpu.SemaphoreType.DMA((head_count - 1,))] * 2,
            compiler_params=pltpu.CompilerParams(
                collective_id=0, has_side_effects=True, vmem_limit_bytes=64 * 1024 * 1024
            ),
            cost_estimate=pl.CostEstimate(
                flops=36 * heads * tokens * size * size, bytes_accessed=16 * tokens * width, transcendentals=0
            ),
        )(
            queries, keys, values, grad_out,
            token_kind.reshape(1, tokens), level_table, head_scale, norm_gain.reshape(1, width),
        )

    in_specs = (
        P("ctx", "head"),
        P("ctx", "head"),
        P("ctx", "head"),
        P("ctx", "head"),
        P("ctx"),
        P(None, "head", None),
        P("head"),
        P("head"),
    )
    return jax.shard_map(
        shards, mesh=mesh, in_specs=in_specs, out_specs=(P("ctx", "head"),) * 4, check_vma=False
    )
```

```python
import functools

import jax
import jax.numpy as jnp
from jax import lax
from jax.experimental import pallas as pl
from jax.experimental.pallas import tpu as pltpu
from jax.sharding import PartitionSpec as P

EPSILON = 1e-06
CHUNK = 2
F32 = jnp.float32
BF16 = jnp.bfloat16


def factor(level):
    return 0.25 * 2.0 ** (-0.5 * level)


def dot(left, right, contract):
    return lax.dot_general(left, right, (contract, ((), ())), preferred_element_type=F32)


NN = ((1,), (0,))
NT = ((1,), (1,))
TN = ((0,), (0,))


def kernel(
    ctx_count, head_count,
    q_hbm, k_hbm, v_hbm, dy_hbm, kind_hbm, table_hbm, scale_hbm, gain_hbm,
    att_hbm, gq_hbm, gk_hbm, gv_hbm,
    q_ref, k_ref, v_ref, dy_ref, kind_ref, table_ref, scale_ref, gain_ref,
    att_ref, gq_ref, gk_ref, gv_ref, kind_col, inv_col, coef_col,
    states, probs, query_t, readout, grad_out_ref, kind_sums, grad_states, key_acc, value_acc,
    own_send, total_send, fwd_recv, half_send, half_recv, back_send, back_recv, last_send, last_recv,
    stat_send, stat_recv,
    load_sem, store_sem, own_ssem, total_ssem, relay_ssem, fwd_rsem, half_ssem, half_rsem,
    back_ssem, back_rsem, last_ssem, last_rsem, stat_ssem, stat_rsem,
):
    tokens, width = q_ref.shape
    heads, size, _ = states.shape
    kinds = table_ref.shape[0]
    depth = ctx_count.bit_length() - 1
    pairs = ctx_count // 2
    half = heads // 2
    parts = half // CHUNK
    c = lax.axis_index("ctx")
    me = lax.axis_index("head")
    pair, side = c >> 1, c & 1
    mesh_id = pl.DeviceIdType.MESH
    odd = side == 1
    inner = pair != pairs - 1
    upper = [((c >> b) & 1) == 1 for b in range(depth)]
    source = [None] + [(pair & ((1 << b) - 1)) == (1 << (b - 1)) - 1 for b in range(1, depth)]
    above = [None] + [
        jnp.logical_and(inner, (pair & ((1 << b) - 1)) == (1 << b) - 1) for b in range(1, depth)
    ]
    place = [None] + [pair & ((1 << (b - 1)) - 1) for b in range(1, depth)]
    origin = [None] + [pair - place[b] - 1 for b in range(1, depth)]
    beside = {"ctx": c ^ 1}

    def at_pair(other):
        return {"ctx": 2 * other + side}

    loads = [
        pltpu.make_async_copy(src, dst, load_sem.at[i])
        for i, (src, dst) in enumerate(
            (
                (k_hbm, k_ref), (v_hbm, v_ref), (q_hbm, q_ref), (dy_hbm, dy_ref),
                (kind_hbm, kind_ref), (table_hbm, table_ref), (scale_hbm, scale_ref), (gain_hbm, gain_ref),
            )
        )
    ]
    for load in loads:
        load.start()

    barrier = pltpu.get_barrier_semaphore()

    def greet(device):
        pl.semaphore_signal(barrier, inc=1, device_id=device, device_id_type=mesh_id)

    greet(beside)
    for d in range(1, head_count):
        greet({"head": lax.rem(me + d, head_count)})
    greeted = head_count
    for b in range(1, depth):

        @pl.when(upper[b])
        def _():
            greet(at_pair(origin[b]))

        @pl.when(source[b])
        def _():
            for t in range(1 << (b - 1)):
                greet(at_pair(pair + 1 + t))

        greeted = greeted + ((c >> b) & 1) + jnp.where(source[b], 1 << (b - 1), 0)

    def first_chunk(mine, jj):
        return (side if mine else 1 - side) * parts + jj

    def chunk_heads(mine, jj):
        first = first_chunk(mine, jj) * CHUNK
        return [first + i for i in range(CHUNK)]

    def part(mine, jj):
        return pl.ds(first_chunk(mine, jj) * CHUNK, CHUNK)

    def cols(h):
        return pl.ds(pl.multiple_of(h * size, size), size)

    def remote(src, dst, ssem, rsem, device):
        return pltpu.make_async_remote_copy(
            src_ref=src, dst_ref=dst, send_sem=ssem, recv_sem=rsem, device_id=device, device_id_type=mesh_id
        )

    def own_copy(mine, jj):
        at, j = part(mine, jj), first_chunk(mine, jj)
        return remote(own_send.at[at], fwd_recv.at[0, at], own_ssem.at[j], fwd_rsem.at[0, j], beside)

    def total_copy(b, t, mine, jj):
        at, j = part(mine, jj), first_chunk(mine, jj)
        return remote(
            total_send.at[at], fwd_recv.at[b, at], total_ssem.at[t, j], fwd_rsem.at[b, j], at_pair(pair + 1 + t)
        )

    def relay_copy(b, mine, jj):
        at, j = part(mine, jj), first_chunk(mine, jj)
        return remote(fwd_recv.at[b, at], fwd_recv.at[b, at], relay_ssem.at[b, j], fwd_rsem.at[b, j], beside)

    def half_copy(b, mine, jj):
        at, j = part(mine, jj), first_chunk(mine, jj)
        return remote(half_send.at[b, at], half_recv.at[b, at], half_ssem.at[b, j], half_rsem.at[b, j], beside)

    def back_copy(b, mine, jj):
        at, j = part(mine, jj), first_chunk(mine, jj)
        return remote(
            back_send.at[b, at], back_recv.at[place[b], at], back_ssem.at[b, j], back_rsem.at[place[b], j],
            at_pair(origin[b]),
        )

    def back_arrival(t, mine, jj):
        at, j = part(mine, jj), first_chunk(mine, jj)
        return remote(back_send.at[0, at], back_recv.at[t, at], back_ssem.at[0, j], back_rsem.at[t, j], beside)

    def last_copy(mine, jj):
        at, j = part(mine, jj), first_chunk(mine, jj)
        return remote(last_send.at[at], last_recv.at[at], last_ssem.at[j], last_rsem.at[j], beside)

    def takes(mine):
        return jnp.logical_or(odd, jnp.logical_and(inner, True if mine else source[1]))

    def gives(mine):
        return jnp.logical_or(side == 0, jnp.logical_and(inner, source[1] if mine else True))

    chunk_list = [(mine, jj) for mine in (False, True) for jj in range(parts)]

    def weight(kind, h, level):
        return table_ref[kind, h, level].astype(F32) * factor(level)

    def token_weights(h, level):
        out = jnp.full((tokens, size), weight(0, h, level), F32)
        for kind in range(1, kinds):
            out = jnp.where(kind_col[...] == kind, weight(kind, h, level), out)
        return out

    def causal():
        row = lax.broadcasted_iota(jnp.int32, (tokens, tokens), 0)
        col = lax.broadcasted_iota(jnp.int32, (tokens, tokens), 1)
        return col <= row

    loads[0].wait()
    loads[1].wait()
    for index, (mine, jj) in enumerate(chunk_list):
        for h in chunk_heads(mine, jj):
            state = dot(k_ref[:, cols(h)], v_ref[:, cols(h)], TN)
            states[h] = state
            own_send[h] = state.astype(BF16)
        if index == 0:
            pl.semaphore_wait(barrier, greeted)

        @pl.when(gives(mine))
        def _():
            own_copy(mine, jj).start()

    for load in loads[2:]:
        load.wait()
    kind_col[...] = jnp.transpose(
        jnp.broadcast_to(kind_ref[...].astype(F32), (size, tokens))
    )

    def local_forward(mine, jj):
        for h in chunk_heads(mine, jj):
            q = q_ref[:, cols(h)]
            scores = dot(q, k_ref[:, cols(h)], NT)
            attn = (jnp.where(causal(), scores, 0.0) * token_weights(h, 0)).astype(BF16)
            probs[h] = attn
            readout[h] = dot(attn, v_ref[:, cols(h)], NN)
            query_t[h] = jnp.transpose(q)

    def send_total(b, mine, jj):
        for h in chunk_heads(mine, jj):
            total_send[h] = states[h].astype(BF16)
        for t in reversed(range(1 << (b - 1))):
            total_copy(b, t, mine, jj).start()

    def add_level(b, mine, jj):
        for h in chunk_heads(mine, jj):
            level = dot(q_ref[:, cols(h)], fwd_recv[b, h], NN)
            readout[h] += token_weights(h, b + 1) * level

    def add_state(b, mine, jj):
        for h in chunk_heads(mine, jj):
            states[h] += fwd_recv[b, h].astype(F32)

    def receive_first(mine, jj):
        @pl.when(takes(mine))
        def _():
            own_copy(mine, jj).wait_recv()
            add_state(0, mine, jj)

        if depth > 1:

            @pl.when(source[1])
            def _():
                send_total(1, mine, jj)

        @pl.when(odd)
        def _():
            add_level(0, mine, jj)

    def receive_total(b, mine, jj):
        @pl.when(upper[b])
        def _():
            total_copy(b, 0, mine, jj).wait_recv()
            if b > 1 and mine:
                relay_copy(b, mine, jj).start()

        if mine and b + 1 < depth:

            @pl.when(above[b])
            def _():
                add_state(b, mine, jj)

            @pl.when(source[b + 1])
            def _():
                send_total(b + 1, mine, jj)

        @pl.when(upper[b])
        def _():
            add_level(b, mine, jj)

    events = []
    stride = 3 * parts + 5
    for jj in range(parts):
        events += [
            (0.5 + jj, local_forward, (True, jj)),
            (0.5 + jj + parts, local_forward, (False, jj)),
            (1.0 + jj, receive_first, (True, jj)),
            (1.0 + jj + parts, receive_first, (False, jj)),
        ]
        if depth > 1:
            events += [
                (2.3 + jj, receive_total, (1, True, jj)),
                (2.3 + jj + parts, receive_total, (1, False, jj)),
            ]
        for b in range(2, depth):
            now = 4.6 + 2 * jj + (b - 2) * stride
            events += [
                (now, receive_total, (b, True, jj)),
                (now + 1.4, receive_total, (b, False, jj)),
            ]
    for _, event, at in sorted(events, key=lambda item: item[0]):
        event(*at)

    squares = jnp.zeros((tokens, size), F32)
    crosses = jnp.zeros((tokens, size), F32)
    for mine, jj in chunk_list:
        for h in chunk_heads(mine, jj):
            z = readout[h] * scale_ref[h]
            readout[h] = z
            squares += z * z
            crosses += gain_ref[:, cols(h)] * dy_ref[:, cols(h)].astype(F32) * z

    stat_send[0:1, :] = jnp.sum(jnp.transpose(squares), axis=0, keepdims=True)
    stat_send[1:2, :] = jnp.sum(jnp.transpose(crosses), axis=0, keepdims=True)
    stat_copies = [
        remote(
            stat_send, stat_recv.at[d - 1], stat_ssem.at[d - 1], stat_rsem.at[d - 1],
            {"head": lax.rem(me + d, head_count)},
        )
        for d in range(1, head_count)
    ]
    for copy in stat_copies:
        copy.start()
    square_row = stat_send[0:1, :]
    cross_row = stat_send[1:2, :]
    for d, copy in enumerate(stat_copies):
        copy.wait_recv()
        square_row += stat_recv[d, 0:1, :]
        cross_row += stat_recv[d, 1:2, :]
    features = width * head_count
    rms = jnp.sqrt(square_row / features + EPSILON)
    coef = cross_row / (features * rms * rms * rms)
    inv_col[...] = jnp.transpose(jnp.broadcast_to(1.0 / rms, (size, tokens)))
    coef_col[...] = jnp.transpose(jnp.broadcast_to(coef, (size, tokens)))

    def message(b, h, flag=1.0):
        total = None
        for kind in range(kinds):
            term = (weight(kind, h, b + 1) * flag) * kind_sums[h, :, pl.ds(kind * size, size)]
            total = term if total is None else total + term
        return total

    def send_bucket_grad(mine, jj):
        for h in chunk_heads(mine, jj):
            back_send[1, h] = (grad_states[h] + message(1, h)).astype(BF16)
        back_copy(1, mine, jj).start()

    for mine, jj in chunk_list:
        for h in chunk_heads(mine, jj):
            gain = gain_ref[:, cols(h)]
            z = readout[h]
            att_ref[:, cols(h)] = (z * inv_col[...] * gain).astype(BF16)
            grad = gain * dy_ref[:, cols(h)].astype(F32) * inv_col[...] - z * coef_col[...]
            grad = (grad * scale_ref[h]).astype(BF16)
            grad_out_ref[h] = grad
            masked = jnp.concatenate(
                [jnp.where(kind_col[...] == kind, grad.astype(F32), 0.0).astype(BF16) for kind in range(kinds)],
                axis=1,
            )
            kind_sums[h] = dot(query_t[h], masked, NN)
            grad_states[h] = jnp.zeros((size, size), F32)
        if not mine:
            for b in reversed(range(2, depth)):

                @pl.when(upper[b])
                def _():
                    for h in chunk_heads(mine, jj):
                        half_send[b, h] = message(b, h).astype(BF16)
                    half_copy(b, mine, jj).start()

        if depth > 1:

            @pl.when(jnp.logical_and(upper[1], jnp.logical_not(above[1])) if mine else upper[1])
            def _():
                send_bucket_grad(mine, jj)

    stores = [
        pltpu.make_async_copy(src, dst, store_sem.at[i])
        for i, (src, dst) in enumerate(
            ((att_ref, att_hbm), (gq_ref, gq_hbm), (gk_ref, gk_hbm), (gv_ref, gv_hbm))
        )
    ]
    stores[0].start()

    def local_backward(mine, jj):
        for h in chunk_heads(mine, jj):
            grad = grad_out_ref[h]
            scores = dot(grad, v_ref[:, cols(h)], NT)
            dprobs = (jnp.where(causal(), scores, 0.0) * token_weights(h, 0)).astype(BF16)
            key_acc[h] = dot(dprobs, q_ref[:, cols(h)], TN)
            value_acc[h] = dot(probs[h], grad, TN)
            readout[h] = dot(dprobs, k_ref[:, cols(h)], NN)
        for b in range(depth):

            @pl.when(upper[b])
            def _():
                for h in chunk_heads(mine, jj):
                    level = dot(grad_out_ref[h], fwd_recv[b, h], NT)
                    readout[h] += token_weights(h, b + 1) * level

        for h in chunk_heads(mine, jj):
            gq_ref[:, cols(h)] = readout[h].astype(BF16)

    def pass_half(b, jj):
        @pl.when(upper[b])
        def _():
            half_copy(b, True, jj).wait_recv()
            for h in chunk_heads(True, jj):
                total = grad_states[h] + message(b, h) + half_recv[b, h].astype(F32)
                back_send[b, h] = total.astype(BF16)
            back_copy(b, True, jj).start()

    def gather_grads(b, mine, jj):
        @pl.when(source[b])
        def _():
            for t in range(1 << (b - 1)):
                back_arrival(t, mine, jj).wait_recv()
                for h in chunk_heads(mine, jj):
                    grad_states[h] += back_recv[t, h].astype(F32)

    def pass_bucket_grad(jj):
        @pl.when(jnp.logical_and(upper[1], above[1]))
        def _():
            send_bucket_grad(True, jj)

    def send_last(mine, jj):
        @pl.when(takes(mine))
        def _():
            flag = side.astype(F32)
            for h in chunk_heads(mine, jj):
                last_send[h] = (grad_states[h] + message(0, h, flag)).astype(BF16)
            last_copy(mine, jj).start()

    def finish(mine, jj):
        @pl.when(gives(mine))
        def _():
            last_copy(mine, jj).wait_recv()
            for h in chunk_heads(mine, jj):
                grad_states[h] += last_recv[h].astype(F32)

        for h in chunk_heads(mine, jj):
            state = grad_states[h].astype(BF16)
            gk_ref[:, cols(h)] = (key_acc[h] + dot(v_ref[:, cols(h)], state, NT)).astype(BF16)
            gv_ref[:, cols(h)] = (value_acc[h] + dot(k_ref[:, cols(h)], state, NN)).astype(BF16)

    events = []
    late = max(depth - 3, 0) * stride
    for jj in range(parts):
        for b in range(2, depth):
            now = (depth - 1 - b) * stride
            events += [
                (now + 1.0 + jj, pass_half, (b, jj)),
                (now + 3.3 + 2 * jj, gather_grads, (b, True, jj)),
            ]
        if depth > 1:
            events += [
                (late + 3.4 + 2 * jj, pass_bucket_grad, (jj,)),
                (late + 2.5 + jj, gather_grads, (1, False, jj)),
                (late + 4.7 + 2 * jj, gather_grads, (1, True, jj)),
            ]
        events += [
            (0.9 + 0.2 * jj, local_backward, (False, jj)),
            (2.3 + 0.2 * jj, local_backward, (True, jj)),
            (late + 2.6 + jj, send_last, (False, jj)),
            (late + 4.8 + 2 * jj, send_last, (True, jj)),
            (late + 5.0 + 2 * jj, finish, (True, jj)),
            (late + 5.9 + 2 * jj, finish, (False, jj)),
        ]
    for _, event, at in sorted(events, key=lambda item: item[0]):
        event(*at)
    for store in stores[1:]:
        store.start()

    for copy in stat_copies:
        copy.wait_send()
    for mine, jj in chunk_list:

        @pl.when(gives(mine))
        def _():
            own_copy(mine, jj).wait_send()

        @pl.when(takes(mine))
        def _():
            last_copy(mine, jj).wait_send()

        for b in range(1, depth):
            if mine or b == 1:

                @pl.when(source[b])
                def _():
                    for t in range(1 << (b - 1)):
                        total_copy(b, t, mine, jj).wait_send()

                @pl.when(upper[b])
                def _():
                    back_copy(b, mine, jj).wait_send()
                    if b > 1:
                        relay_copy(b, mine, jj).wait_send()

            else:

                @pl.when(upper[b])
                def _():
                    half_copy(b, mine, jj).wait_send()

    for store in stores:
        store.wait()


def land(*refs):
    count = (len(refs) - 1) // 2
    copies = [
        pltpu.make_async_copy(refs[i], refs[count + i], refs[-1].at[i]) for i in range(count)
    ]
    for copy in copies:
        copy.start()
    for copy in copies:
        copy.wait()


def solution(mesh):
    ctx_count, head_count = mesh.shape["ctx"], mesh.shape["head"]
    depth = ctx_count.bit_length() - 1
    targets = max(ctx_count // 4, 1)

    def shards(queries, keys, values, grad_out, token_kind, level_table, head_scale, norm_gain):
        tokens, width = queries.shape
        kinds, heads, _ = level_table.shape
        size = width // heads
        chunks = heads // CHUNK
        hbm = pl.BlockSpec(memory_space=pltpu.HBM)
        block = jax.ShapeDtypeStruct((tokens, width), BF16)
        square = (heads, size, size)
        dma = pltpu.SemaphoreType.DMA
        results = pl.pallas_call(
            functools.partial(kernel, ctx_count, head_count),
            out_shape=(block,) * 4,
            in_specs=[hbm] * 8,
            out_specs=(hbm,) * 4,
            scratch_shapes=[pltpu.VMEM((tokens, width), BF16)] * 4
            + [
                pltpu.VMEM((1, tokens), jnp.int32),
                pltpu.SMEM(level_table.shape, jnp.int32),
                pltpu.SMEM((heads,), F32),
                pltpu.VMEM((1, width), F32),
            ]
            + [pltpu.VMEM((tokens, width), BF16)] * 4
            + [pltpu.VMEM((tokens, size), F32)] * 3
            + [
                pltpu.VMEM(square, F32),
                pltpu.VMEM((heads, tokens, tokens), BF16),
                pltpu.VMEM((heads, size, tokens), BF16),
                pltpu.VMEM((heads, tokens, size), F32),
                pltpu.VMEM((heads, tokens, size), BF16),
                pltpu.VMEM((heads, size, kinds * size), F32),
                pltpu.VMEM(square, F32),
                pltpu.VMEM((heads, tokens, size), F32),
                pltpu.VMEM((heads, tokens, size), F32),
                pltpu.VMEM(square, BF16),
                pltpu.VMEM(square, BF16),
                pltpu.VMEM((depth,) + square, BF16),
                pltpu.VMEM((depth,) + square, BF16),
                pltpu.VMEM((depth,) + square, BF16),
                pltpu.VMEM((depth,) + square, BF16),
                pltpu.VMEM((targets,) + square, BF16),
                pltpu.VMEM(square, BF16),
                pltpu.VMEM(square, BF16),
                pltpu.VMEM((8, tokens), F32),
                pltpu.VMEM((head_count - 1, 8, tokens), F32),
                dma((8,)),
                dma((4,)),
                dma((chunks,)),
                dma((targets, chunks)),
                dma((depth, chunks)),
                dma((depth, chunks)),
                dma((depth, chunks)),
                dma((depth, chunks)),
                dma((depth, chunks)),
                dma((targets, chunks)),
                dma((chunks,)),
                dma((chunks,)),
                dma((head_count - 1,)),
                dma((head_count - 1,)),
            ],
            compiler_params=pltpu.CompilerParams(
                collective_id=0, has_side_effects=True, vmem_limit_bytes=64 * 1024 * 1024
            ),
            cost_estimate=pl.CostEstimate(
                flops=36 * heads * tokens * size * size, bytes_accessed=16 * tokens * width, transcendentals=0
            ),
        )(
            queries, keys, values, grad_out,
            token_kind.reshape(1, tokens), level_table, head_scale, norm_gain.reshape(1, width),
        )
        return pl.pallas_call(
            land,
            out_shape=(block,) * 4,
            in_specs=[hbm] * 4,
            out_specs=(hbm,) * 4,
            scratch_shapes=[dma((4,))],
            compiler_params=pltpu.CompilerParams(vmem_limit_bytes=64 * 1024 * 1024),
        )(*results)

    in_specs = (
        P("ctx", "head"),
        P("ctx", "head"),
        P("ctx", "head"),
        P("ctx", "head"),
        P("ctx"),
        P(None, "head", None),
        P("head"),
        P("head"),
    )
    return jax.shard_map(
        shards, mesh=mesh, in_specs=in_specs, out_specs=(P("ctx", "head"),) * 4, check_vma=False
    )
```

```python
import functools

import jax
import jax.numpy as jnp
from jax import lax
from jax.experimental import pallas as pl
from jax.experimental.pallas import tpu as pltpu
from jax.sharding import PartitionSpec as P

EPSILON = 1e-06
CHUNK = 1
GROUP = 2
F32 = jnp.float32
BF16 = jnp.bfloat16


def factor(level):
    return 0.25 * 2.0 ** (-0.5 * level)


def dot(left, right, contract):
    return lax.dot_general(left, right, (contract, ((), ())), preferred_element_type=F32)


NN = ((1,), (0,))
NT = ((1,), (1,))
TN = ((0,), (0,))


def kernel(
    ctx_count, head_count,
    q_hbm, k_hbm, v_hbm, dy_hbm, kind_hbm, table_hbm, scale_hbm, gain_hbm,
    att_hbm, gq_hbm, gk_hbm, gv_hbm,
    q_ref, k_ref, v_ref, dy_ref, kind_ref, table_ref, scale_ref, gain_ref,
    att_ref, gq_ref, gk_ref, gv_ref, kind_col, inv_col, coef_col,
    states, probs, query_t, readout, grad_out_ref, kind_sums, grad_states, key_acc, value_acc,
    own_send, total_send, fwd_recv, half_send, half_recv, back_send, back_recv, last_send, last_recv,
    stat_send, stat_recv,
    load_sem, store_sem, own_ssem, total_ssem, relay_ssem, fwd_rsem, half_ssem, half_rsem,
    back_ssem, back_rsem, last_ssem, last_rsem, stat_ssem, stat_rsem,
):
    tokens, width = q_ref.shape
    heads, size, _ = states.shape
    kinds = table_ref.shape[0]
    depth = ctx_count.bit_length() - 1
    pairs = ctx_count // 2
    half = heads // 2
    parts = half // CHUNK
    c = lax.axis_index("ctx")
    me = lax.axis_index("head")
    pair, side = c >> 1, c & 1
    mesh_id = pl.DeviceIdType.MESH
    odd = side == 1
    inner = pair != pairs - 1
    upper = [((c >> b) & 1) == 1 for b in range(depth)]
    source = [None] + [(pair & ((1 << b) - 1)) == (1 << (b - 1)) - 1 for b in range(1, depth)]
    above = [None] + [
        jnp.logical_and(inner, (pair & ((1 << b) - 1)) == (1 << b) - 1) for b in range(1, depth)
    ]
    place = [None] + [pair & ((1 << (b - 1)) - 1) for b in range(1, depth)]
    origin = [None] + [pair - place[b] - 1 for b in range(1, depth)]
    beside = {"ctx": c ^ 1}

    def at_pair(other):
        return {"ctx": 2 * other + side}

    loads = [
        pltpu.make_async_copy(src, dst, load_sem.at[i])
        for i, (src, dst) in enumerate(
            (
                (k_hbm, k_ref), (v_hbm, v_ref), (q_hbm, q_ref), (dy_hbm, dy_ref),
                (kind_hbm, kind_ref), (table_hbm, table_ref), (scale_hbm, scale_ref), (gain_hbm, gain_ref),
            )
        )
    ]
    for load in loads:
        load.start()

    barrier = pltpu.get_barrier_semaphore()

    def greet(device):
        pl.semaphore_signal(barrier, inc=1, device_id=device, device_id_type=mesh_id)

    greet(beside)
    for d in range(1, head_count):
        greet({"head": lax.rem(me + d, head_count)})
    greeted = head_count
    for b in range(1, depth):

        @pl.when(upper[b])
        def _():
            greet(at_pair(origin[b]))

        @pl.when(source[b])
        def _():
            for t in range(1 << (b - 1)):
                greet(at_pair(pair + 1 + t))

        greeted = greeted + ((c >> b) & 1) + jnp.where(source[b], 1 << (b - 1), 0)

    def first_chunk(mine, jj):
        return (side if mine else 1 - side) * parts + jj

    def chunk_heads(mine, *several):
        return [first_chunk(mine, jj) * CHUNK + i for jj in several for i in range(CHUNK)]

    def part(mine, jj):
        return pl.ds(first_chunk(mine, jj) * CHUNK, CHUNK)

    def cols(h):
        return pl.ds(pl.multiple_of(h * size, size), size)

    def remote(src, dst, ssem, rsem, device):
        return pltpu.make_async_remote_copy(
            src_ref=src, dst_ref=dst, send_sem=ssem, recv_sem=rsem, device_id=device, device_id_type=mesh_id
        )

    def own_copy(mine, jj):
        at, j = part(mine, jj), first_chunk(mine, jj)
        return remote(own_send.at[at], fwd_recv.at[0, at], own_ssem.at[j], fwd_rsem.at[0, j], beside)

    def total_copy(b, t, mine, jj):
        at, j = part(mine, jj), first_chunk(mine, jj)
        return remote(
            total_send.at[at], fwd_recv.at[b, at], total_ssem.at[t, j], fwd_rsem.at[b, j], at_pair(pair + 1 + t)
        )

    def relay_copy(b, mine, jj):
        at, j = part(mine, jj), first_chunk(mine, jj)
        return remote(fwd_recv.at[b, at], fwd_recv.at[b, at], relay_ssem.at[b, j], fwd_rsem.at[b, j], beside)

    def half_copy(b, mine, jj):
        at, j = part(mine, jj), first_chunk(mine, jj)
        return remote(half_send.at[b, at], half_recv.at[b, at], half_ssem.at[b, j], half_rsem.at[b, j], beside)

    def back_copy(b, mine, jj):
        at, j = part(mine, jj), first_chunk(mine, jj)
        return remote(
            back_send.at[b, at], back_recv.at[place[b], at], back_ssem.at[b, j], back_rsem.at[place[b], j],
            at_pair(origin[b]),
        )

    def back_arrival(t, mine, jj):
        at, j = part(mine, jj), first_chunk(mine, jj)
        return remote(back_send.at[0, at], back_recv.at[t, at], back_ssem.at[0, j], back_rsem.at[t, j], beside)

    def last_copy(mine, jj):
        at, j = part(mine, jj), first_chunk(mine, jj)
        return remote(last_send.at[at], last_recv.at[at], last_ssem.at[j], last_rsem.at[j], beside)

    def takes(mine):
        return jnp.logical_or(odd, jnp.logical_and(inner, True if mine else source[1]))

    def gives(mine):
        return jnp.logical_or(side == 0, jnp.logical_and(inner, source[1] if mine else True))

    chunk_list = [(mine, jj) for mine in (False, True) for jj in range(parts)]
    groups = [tuple(range(jj, min(jj + GROUP, parts))) for jj in range(0, parts, GROUP)]

    def weight(kind, h, level):
        return table_ref[kind, h, level].astype(F32) * factor(level)

    def token_weights(h, level):
        out = jnp.full((tokens, size), weight(0, h, level), F32)
        for kind in range(1, kinds):
            out = jnp.where(kind_col[...] == kind, weight(kind, h, level), out)
        return out

    def causal():
        row = lax.broadcasted_iota(jnp.int32, (tokens, tokens), 0)
        col = lax.broadcasted_iota(jnp.int32, (tokens, tokens), 1)
        return col <= row

    loads[0].wait()
    loads[1].wait()
    for index, (mine, jj) in enumerate(chunk_list):
        for h in chunk_heads(mine, jj):
            state = dot(k_ref[:, cols(h)], v_ref[:, cols(h)], TN)
            states[h] = state
            own_send[h] = state.astype(BF16)
        if index == 0:
            pl.semaphore_wait(barrier, greeted)

        @pl.when(gives(mine))
        def _():
            own_copy(mine, jj).start()

    for load in loads[2:]:
        load.wait()
    kind_col[...] = jnp.transpose(
        jnp.broadcast_to(kind_ref[...].astype(F32), (size, tokens))
    )

    def local_forward(mine, group):
        for h in chunk_heads(mine, *group):
            q = q_ref[:, cols(h)]
            scores = dot(q, k_ref[:, cols(h)], NT)
            attn = (jnp.where(causal(), scores, 0.0) * token_weights(h, 0)).astype(BF16)
            probs[h] = attn
            readout[h] = dot(attn, v_ref[:, cols(h)], NN)
            query_t[h] = jnp.transpose(q)

    def send_total(b, mine, jj):
        for h in chunk_heads(mine, jj):
            total_send[h] = states[h].astype(BF16)
        for t in reversed(range(1 << (b - 1))):
            total_copy(b, t, mine, jj).start()

    def add_level(b, mine, group):
        @pl.when(upper[b])
        def _():
            for h in chunk_heads(mine, *group):
                level = dot(q_ref[:, cols(h)], fwd_recv[b, h], NN)
                readout[h] += token_weights(h, b + 1) * level

    def add_state(b, mine, jj):
        for h in chunk_heads(mine, jj):
            states[h] += fwd_recv[b, h].astype(F32)

    def receive_first(mine, jj):
        @pl.when(takes(mine))
        def _():
            own_copy(mine, jj).wait_recv()
            add_state(0, mine, jj)

        if depth > 1:

            @pl.when(source[1])
            def _():
                send_total(1, mine, jj)

    def receive_total(b, mine, jj):
        @pl.when(upper[b])
        def _():
            total_copy(b, 0, mine, jj).wait_recv()
            if b > 1 and mine:
                relay_copy(b, mine, jj).start()

        if mine and b + 1 < depth:

            @pl.when(above[b])
            def _():
                add_state(b, mine, jj)

            @pl.when(source[b + 1])
            def _():
                send_total(b + 1, mine, jj)

    events = []
    stride = 3 * parts + 5
    for mine in (True, False):
        skip = 0 if mine else parts
        for group in groups:
            events += [
                (0.5 + group[0] + skip, local_forward, (mine, group)),
                (1.4 + group[-1] + skip, add_level, (0, mine, group)),
            ]
            if depth > 1:
                events += [(2.7 + group[-1] + skip, add_level, (1, mine, group))]
            for b in range(2, depth):
                now = 4.6 + 2 * group[-1] + (b - 2) * stride + (0 if mine else 1.4)
                events += [(now + 0.1, add_level, (b, mine, group))]
        for jj in range(parts):
            events += [(1.0 + jj + skip, receive_first, (mine, jj))]
            if depth > 1:
                events += [(2.3 + jj + skip, receive_total, (1, mine, jj))]
            for b in range(2, depth):
                now = 4.6 + 2 * jj + (b - 2) * stride + (0 if mine else 1.4)
                events += [(now, receive_total, (b, mine, jj))]
    for _, event, at in sorted(events, key=lambda item: item[0]):
        event(*at)

    squares = jnp.zeros((tokens, size), F32)
    crosses = jnp.zeros((tokens, size), F32)
    for mine, jj in chunk_list:
        for h in chunk_heads(mine, jj):
            z = readout[h] * scale_ref[h]
            readout[h] = z
            squares += z * z
            crosses += gain_ref[:, cols(h)] * dy_ref[:, cols(h)].astype(F32) * z

    stat_send[0:1, :] = jnp.sum(jnp.transpose(squares), axis=0, keepdims=True)
    stat_send[1:2, :] = jnp.sum(jnp.transpose(crosses), axis=0, keepdims=True)
    stat_copies = [
        remote(
            stat_send, stat_recv.at[d - 1], stat_ssem.at[d - 1], stat_rsem.at[d - 1],
            {"head": lax.rem(me + d, head_count)},
        )
        for d in range(1, head_count)
    ]
    for copy in stat_copies:
        copy.start()
    square_row = stat_send[0:1, :]
    cross_row = stat_send[1:2, :]
    for d, copy in enumerate(stat_copies):
        copy.wait_recv()
        square_row += stat_recv[d, 0:1, :]
        cross_row += stat_recv[d, 1:2, :]
    features = width * head_count
    rms = jnp.sqrt(square_row / features + EPSILON)
    coef = cross_row / (features * rms * rms * rms)
    inv_col[...] = jnp.transpose(jnp.broadcast_to(1.0 / rms, (size, tokens)))
    coef_col[...] = jnp.transpose(jnp.broadcast_to(coef, (size, tokens)))

    def message(b, h, flag=1.0):
        total = None
        for kind in range(kinds):
            term = (weight(kind, h, b + 1) * flag) * kind_sums[h, :, pl.ds(kind * size, size)]
            total = term if total is None else total + term
        return total

    def send_bucket_grad(mine, jj):
        for h in chunk_heads(mine, jj):
            back_send[1, h] = (grad_states[h] + message(1, h)).astype(BF16)
        back_copy(1, mine, jj).start()

    for mine, group in [(mine, group) for mine in (False, True) for group in groups]:
        for h in chunk_heads(mine, *group):
            gain = gain_ref[:, cols(h)]
            z = readout[h]
            att_ref[:, cols(h)] = (z * inv_col[...] * gain).astype(BF16)
            grad = gain * dy_ref[:, cols(h)].astype(F32) * inv_col[...] - z * coef_col[...]
            grad = (grad * scale_ref[h]).astype(BF16)
            grad_out_ref[h] = grad
            masked = jnp.concatenate(
                [jnp.where(kind_col[...] == kind, grad.astype(F32), 0.0).astype(BF16) for kind in range(kinds)],
                axis=1,
            )
            kind_sums[h] = dot(query_t[h], masked, NN)
            grad_states[h] = jnp.zeros((size, size), F32)
        if not mine:
            for b in reversed(range(2, depth)):

                @pl.when(upper[b])
                def _():
                    for jj in group:
                        for h in chunk_heads(mine, jj):
                            half_send[b, h] = message(b, h).astype(BF16)
                        half_copy(b, mine, jj).start()

        if depth > 1:

            @pl.when(jnp.logical_and(upper[1], jnp.logical_not(above[1])) if mine else upper[1])
            def _():
                for jj in group:
                    send_bucket_grad(mine, jj)

    stores = [
        pltpu.make_async_copy(src, dst, store_sem.at[i])
        for i, (src, dst) in enumerate(
            ((att_ref, att_hbm), (gq_ref, gq_hbm), (gk_ref, gk_hbm), (gv_ref, gv_hbm))
        )
    ]
    stores[0].start()

    def local_backward(mine, group):
        for h in chunk_heads(mine, *group):
            grad = grad_out_ref[h]
            scores = dot(grad, v_ref[:, cols(h)], NT)
            dprobs = (jnp.where(causal(), scores, 0.0) * token_weights(h, 0)).astype(BF16)
            key_acc[h] = dot(dprobs, q_ref[:, cols(h)], TN)
            value_acc[h] = dot(probs[h], grad, TN)
            readout[h] = dot(dprobs, k_ref[:, cols(h)], NN)
        for b in range(depth):

            @pl.when(upper[b])
            def _():
                for h in chunk_heads(mine, *group):
                    level = dot(grad_out_ref[h], fwd_recv[b, h], NT)
                    readout[h] += token_weights(h, b + 1) * level

        for h in chunk_heads(mine, *group):
            gq_ref[:, cols(h)] = readout[h].astype(BF16)

    def pass_half(b, jj):
        @pl.when(upper[b])
        def _():
            half_copy(b, True, jj).wait_recv()
            for h in chunk_heads(True, jj):
                total = grad_states[h] + message(b, h) + half_recv[b, h].astype(F32)
                back_send[b, h] = total.astype(BF16)
            back_copy(b, True, jj).start()

    def gather_grads(b, mine, jj):
        @pl.when(source[b])
        def _():
            for t in range(1 << (b - 1)):
                back_arrival(t, mine, jj).wait_recv()
                for h in chunk_heads(mine, jj):
                    grad_states[h] += back_recv[t, h].astype(F32)

    def pass_bucket_grad(jj):
        @pl.when(jnp.logical_and(upper[1], above[1]))
        def _():
            send_bucket_grad(True, jj)

    def send_last(mine, jj):
        @pl.when(takes(mine))
        def _():
            flag = side.astype(F32)
            for h in chunk_heads(mine, jj):
                last_send[h] = (grad_states[h] + message(0, h, flag)).astype(BF16)
            last_copy(mine, jj).start()

    def finish(mine, jj):
        @pl.when(gives(mine))
        def _():
            last_copy(mine, jj).wait_recv()
            for h in chunk_heads(mine, jj):
                grad_states[h] += last_recv[h].astype(F32)

        for h in chunk_heads(mine, jj):
            state = grad_states[h].astype(BF16)
            gk_ref[:, cols(h)] = (key_acc[h] + dot(v_ref[:, cols(h)], state, NT)).astype(BF16)
            gv_ref[:, cols(h)] = (value_acc[h] + dot(k_ref[:, cols(h)], state, NN)).astype(BF16)

    events = []
    late = max(depth - 3, 0) * stride
    for group in groups:
        events += [
            (0.9 + group[0], local_backward, (False, group)),
            (4.9 + 0.5 * group[0], local_backward, (True, group)),
        ]
    for jj in range(parts):
        for b in range(2, depth):
            now = (depth - 1 - b) * stride
            events += [
                (now + 1.0 + jj, pass_half, (b, jj)),
                (now + 3.3 + 2 * jj, gather_grads, (b, True, jj)),
            ]
        if depth > 1:
            events += [
                (late + 3.4 + 2 * jj, pass_bucket_grad, (jj,)),
                (late + 2.5 + jj, gather_grads, (1, False, jj)),
                (late + 4.7 + 2 * jj, gather_grads, (1, True, jj)),
            ]
        events += [
            (late + 2.6 + jj, send_last, (False, jj)),
            (late + 4.8 + 2 * jj, send_last, (True, jj)),
            (late + 5.0 + 2 * jj, finish, (True, jj)),
            (late + 5.9 + 2 * jj, finish, (False, jj)),
        ]
    for _, event, at in sorted(events, key=lambda item: item[0]):
        event(*at)
    for store in stores[1:]:
        store.start()

    for copy in stat_copies:
        copy.wait_send()
    for mine, jj in chunk_list:

        @pl.when(gives(mine))
        def _():
            own_copy(mine, jj).wait_send()

        @pl.when(takes(mine))
        def _():
            last_copy(mine, jj).wait_send()

        for b in range(1, depth):
            if mine or b == 1:

                @pl.when(source[b])
                def _():
                    for t in range(1 << (b - 1)):
                        total_copy(b, t, mine, jj).wait_send()

                @pl.when(upper[b])
                def _():
                    back_copy(b, mine, jj).wait_send()
                    if b > 1:
                        relay_copy(b, mine, jj).wait_send()

            else:

                @pl.when(upper[b])
                def _():
                    half_copy(b, mine, jj).wait_send()

    for store in stores:
        store.wait()


def land(*refs):
    count = len(refs) // 2
    for source, target in zip(refs[:count], refs[count:]):
        target[...] = source[...]


def solution(mesh):
    ctx_count, head_count = mesh.shape["ctx"], mesh.shape["head"]
    depth = ctx_count.bit_length() - 1
    targets = max(ctx_count // 4, 1)

    def shards(queries, keys, values, grad_out, token_kind, level_table, head_scale, norm_gain):
        tokens, width = queries.shape
        kinds, heads, _ = level_table.shape
        size = width // heads
        chunks = heads // CHUNK
        hbm = pl.BlockSpec(memory_space=pltpu.HBM)
        block = jax.ShapeDtypeStruct((tokens, width), BF16)
        square = (heads, size, size)
        dma = pltpu.SemaphoreType.DMA
        results = pl.pallas_call(
            functools.partial(kernel, ctx_count, head_count),
            out_shape=(block,) * 4,
            in_specs=[hbm] * 8,
            out_specs=(hbm,) * 4,
            scratch_shapes=[pltpu.VMEM((tokens, width), BF16)] * 4
            + [
                pltpu.VMEM((1, tokens), jnp.int32),
                pltpu.SMEM(level_table.shape, jnp.int32),
                pltpu.SMEM((heads,), F32),
                pltpu.VMEM((1, width), F32),
            ]
            + [pltpu.VMEM((tokens, width), BF16)] * 4
            + [pltpu.VMEM((tokens, size), F32)] * 3
            + [
                pltpu.VMEM(square, F32),
                pltpu.VMEM((heads, tokens, tokens), BF16),
                pltpu.VMEM((heads, size, tokens), BF16),
                pltpu.VMEM((heads, tokens, size), F32),
                pltpu.VMEM((heads, tokens, size), BF16),
                pltpu.VMEM((heads, size, kinds * size), F32),
                pltpu.VMEM(square, F32),
                pltpu.VMEM((heads, tokens, size), F32),
                pltpu.VMEM((heads, tokens, size), F32),
                pltpu.VMEM(square, BF16),
                pltpu.VMEM(square, BF16),
                pltpu.VMEM((depth,) + square, BF16),
                pltpu.VMEM((depth,) + square, BF16),
                pltpu.VMEM((depth,) + square, BF16),
                pltpu.VMEM((depth,) + square, BF16),
                pltpu.VMEM((targets,) + square, BF16),
                pltpu.VMEM(square, BF16),
                pltpu.VMEM(square, BF16),
                pltpu.VMEM((8, tokens), F32),
                pltpu.VMEM((head_count - 1, 8, tokens), F32),
                dma((8,)),
                dma((4,)),
                dma((chunks,)),
                dma((targets, chunks)),
                dma((depth, chunks)),
                dma((depth, chunks)),
                dma((depth, chunks)),
                dma((depth, chunks)),
                dma((depth, chunks)),
                dma((targets, chunks)),
                dma((chunks,)),
                dma((chunks,)),
                dma((head_count - 1,)),
                dma((head_count - 1,)),
            ],
            compiler_params=pltpu.CompilerParams(
                collective_id=0, has_side_effects=True, vmem_limit_bytes=64 * 1024 * 1024
            ),
            cost_estimate=pl.CostEstimate(
                flops=36 * heads * tokens * size * size, bytes_accessed=16 * tokens * width, transcendentals=0
            ),
        )(
            queries, keys, values, grad_out,
            token_kind.reshape(1, tokens), level_table, head_scale, norm_gain.reshape(1, width),
        )
        rows = pl.BlockSpec((tokens // 2, width), lambda i: (i, 0))
        return pl.pallas_call(
            land,
            out_shape=(block,) * 4,
            grid=(2,),
            in_specs=[rows] * 4,
            out_specs=(rows,) * 4,
            compiler_params=pltpu.CompilerParams(vmem_limit_bytes=64 * 1024 * 1024),
        )(*results)

    in_specs = (
        P("ctx", "head"),
        P("ctx", "head"),
        P("ctx", "head"),
        P("ctx", "head"),
        P("ctx"),
        P(None, "head", None),
        P("head"),
        P("head"),
    )
    return jax.shard_map(
        shards, mesh=mesh, in_specs=in_specs, out_specs=(P("ctx", "head"),) * 4, check_vma=False
    )
```

```python
import functools

import jax
import jax.numpy as jnp
from jax import lax
from jax.experimental import pallas as pl
from jax.experimental.pallas import tpu as pltpu
from jax.sharding import PartitionSpec as P

EPSILON = 1e-06
CHUNK = 4
GROUP = 1
F32 = jnp.float32
BF16 = jnp.bfloat16


def factor(level):
    return 0.25 * 2.0 ** (-0.5 * level)


def dot(left, right, contract):
    return lax.dot_general(left, right, (contract, ((), ())), preferred_element_type=F32)


NN = ((1,), (0,))
NT = ((1,), (1,))
TN = ((0,), (0,))


def kernel(
    ctx_count, head_count,
    q_hbm, k_hbm, v_hbm, dy_hbm, kind_hbm, table_hbm, scale_hbm, gain_hbm,
    att_hbm, gq_hbm, gk_hbm, gv_hbm,
    q_ref, k_ref, v_ref, dy_ref, kind_ref, table_ref, scale_ref, gain_ref,
    att_ref, gq_ref, gk_ref, gv_ref, kind_col, inv_col, coef_col,
    states, probs, query_t, readout, grad_out_ref, kind_sums, grad_states, key_acc, value_acc,
    own_send, total_send, fwd_recv, half_send, half_recv, back_send, back_recv, last_send, last_recv,
    stat_send, stat_recv,
    load_sem, store_sem, own_ssem, total_ssem, relay_ssem, fwd_rsem, half_ssem, half_rsem,
    back_ssem, back_rsem, last_ssem, last_rsem, stat_ssem, stat_rsem,
):
    tokens, width = q_ref.shape
    heads, size, _ = states.shape
    kinds = table_ref.shape[0]
    depth = ctx_count.bit_length() - 1
    pairs = ctx_count // 2
    half = heads // 2
    parts = half // CHUNK
    c = lax.axis_index("ctx")
    me = lax.axis_index("head")
    pair, side = c >> 1, c & 1
    mesh_id = pl.DeviceIdType.MESH
    odd = side == 1
    inner = pair != pairs - 1
    upper = [((c >> b) & 1) == 1 for b in range(depth)]
    source = [None] + [(pair & ((1 << b) - 1)) == (1 << (b - 1)) - 1 for b in range(1, depth)]
    above = [None] + [
        jnp.logical_and(inner, (pair & ((1 << b) - 1)) == (1 << b) - 1) for b in range(1, depth)
    ]
    place = [None] + [pair & ((1 << (b - 1)) - 1) for b in range(1, depth)]
    origin = [None] + [pair - place[b] - 1 for b in range(1, depth)]
    beside = {"ctx": c ^ 1}

    def at_pair(other):
        return {"ctx": 2 * other + side}

    loads = [
        pltpu.make_async_copy(src, dst, load_sem.at[i])
        for i, (src, dst) in enumerate(
            (
                (k_hbm, k_ref), (v_hbm, v_ref), (q_hbm, q_ref), (dy_hbm, dy_ref),
                (kind_hbm, kind_ref), (table_hbm, table_ref), (scale_hbm, scale_ref), (gain_hbm, gain_ref),
            )
        )
    ]
    for load in loads:
        load.start()

    barrier = pltpu.get_barrier_semaphore()

    def greet(device):
        pl.semaphore_signal(barrier, inc=1, device_id=device, device_id_type=mesh_id)

    greet(beside)
    for d in range(1, head_count):
        greet({"head": lax.rem(me + d, head_count)})
    greeted = head_count
    for b in range(1, depth):

        @pl.when(upper[b])
        def _():
            greet(at_pair(origin[b]))

        @pl.when(source[b])
        def _():
            for t in range(1 << (b - 1)):
                greet(at_pair(pair + 1 + t))

        greeted = greeted + ((c >> b) & 1) + jnp.where(source[b], 1 << (b - 1), 0)

    def first_chunk(mine, jj):
        return (side if mine else 1 - side) * parts + jj

    def chunk_heads(mine, *several):
        return [first_chunk(mine, jj) * CHUNK + i for jj in several for i in range(CHUNK)]

    def part(mine, jj):
        return pl.ds(first_chunk(mine, jj) * CHUNK, CHUNK)

    def cols(h):
        return pl.ds(pl.multiple_of(h * size, size), size)

    def remote(src, dst, ssem, rsem, device):
        return pltpu.make_async_remote_copy(
            src_ref=src, dst_ref=dst, send_sem=ssem, recv_sem=rsem, device_id=device, device_id_type=mesh_id
        )

    def own_copy(mine, jj):
        at, j = part(mine, jj), first_chunk(mine, jj)
        return remote(own_send.at[at], fwd_recv.at[0, at], own_ssem.at[j], fwd_rsem.at[0, j], beside)

    def total_copy(b, t, mine, jj):
        at, j = part(mine, jj), first_chunk(mine, jj)
        return remote(
            total_send.at[at], fwd_recv.at[b, at], total_ssem.at[t, j], fwd_rsem.at[b, j], at_pair(pair + 1 + t)
        )

    def relay_copy(b, mine, jj):
        at, j = part(mine, jj), first_chunk(mine, jj)
        return remote(fwd_recv.at[b, at], fwd_recv.at[b, at], relay_ssem.at[b, j], fwd_rsem.at[b, j], beside)

    def half_copy(b, mine, jj):
        at, j = part(mine, jj), first_chunk(mine, jj)
        return remote(half_send.at[b, at], half_recv.at[b, at], half_ssem.at[b, j], half_rsem.at[b, j], beside)

    def back_copy(b, mine, jj):
        at, j = part(mine, jj), first_chunk(mine, jj)
        return remote(
            back_send.at[b, at], back_recv.at[place[b], at], back_ssem.at[b, j], back_rsem.at[place[b], j],
            at_pair(origin[b]),
        )

    def back_arrival(t, mine, jj):
        at, j = part(mine, jj), first_chunk(mine, jj)
        return remote(back_send.at[0, at], back_recv.at[t, at], back_ssem.at[0, j], back_rsem.at[t, j], beside)

    def last_copy(mine, jj):
        at, j = part(mine, jj), first_chunk(mine, jj)
        return remote(last_send.at[at], last_recv.at[at], last_ssem.at[j], last_rsem.at[j], beside)

    def takes(mine):
        return jnp.logical_or(odd, jnp.logical_and(inner, True if mine else source[1]))

    def gives(mine):
        return jnp.logical_or(side == 0, jnp.logical_and(inner, source[1] if mine else True))

    chunk_list = [(mine, jj) for mine in (False, True) for jj in range(parts)]
    groups = [tuple(range(jj, min(jj + GROUP, parts))) for jj in range(0, parts, GROUP)]

    def weight(kind, h, level):
        return table_ref[kind, h, level].astype(F32) * factor(level)

    def token_weights(h, level):
        out = jnp.full((tokens, size), weight(0, h, level), F32)
        for kind in range(1, kinds):
            out = jnp.where(kind_col[...] == kind, weight(kind, h, level), out)
        return out

    def causal():
        row = lax.broadcasted_iota(jnp.int32, (tokens, tokens), 0)
        col = lax.broadcasted_iota(jnp.int32, (tokens, tokens), 1)
        return col <= row

    loads[0].wait()
    loads[1].wait()
    for index, (mine, jj) in enumerate(chunk_list):
        for h in chunk_heads(mine, jj):
            state = dot(k_ref[:, cols(h)], v_ref[:, cols(h)], TN)
            states[h] = state
            own_send[h] = state.astype(BF16)
        if index == 0:
            pl.semaphore_wait(barrier, greeted)

        @pl.when(gives(mine))
        def _():
            own_copy(mine, jj).start()

    for load in loads[2:]:
        load.wait()
    kind_col[...] = jnp.transpose(
        jnp.broadcast_to(kind_ref[...].astype(F32), (size, tokens))
    )

    def local_forward(mine, group):
        for h in chunk_heads(mine, *group):
            q = q_ref[:, cols(h)]
            scores = dot(q, k_ref[:, cols(h)], NT)
            attn = (jnp.where(causal(), scores, 0.0) * token_weights(h, 0)).astype(BF16)
            probs[h] = attn
            readout[h] = dot(attn, v_ref[:, cols(h)], NN)
            query_t[h] = jnp.transpose(q)

    def send_total(b, mine, jj):
        for h in chunk_heads(mine, jj):
            total_send[h] = states[h].astype(BF16)
        for t in reversed(range(1 << (b - 1))):
            total_copy(b, t, mine, jj).start()

    def add_level(b, mine, group):
        @pl.when(upper[b])
        def _():
            for h in chunk_heads(mine, *group):
                level = dot(q_ref[:, cols(h)], fwd_recv[b, h], NN)
                readout[h] += token_weights(h, b + 1) * level

    def add_state(b, mine, jj):
        for h in chunk_heads(mine, jj):
            states[h] += fwd_recv[b, h].astype(F32)

    def receive_first(mine, jj):
        @pl.when(takes(mine))
        def _():
            own_copy(mine, jj).wait_recv()
            add_state(0, mine, jj)

        if depth > 1:

            @pl.when(source[1])
            def _():
                send_total(1, mine, jj)

    def receive_total(b, mine, jj):
        @pl.when(upper[b])
        def _():
            total_copy(b, 0, mine, jj).wait_recv()
            if b > 1 and mine:
                relay_copy(b, mine, jj).start()

        if mine and b + 1 < depth:

            @pl.when(above[b])
            def _():
                add_state(b, mine, jj)

            @pl.when(source[b + 1])
            def _():
                send_total(b + 1, mine, jj)

    events = []
    stride = 3 * parts + 5
    for mine in (True, False):
        skip = 0 if mine else parts
        for group in groups:
            events += [
                (0.5 + group[0] + skip, local_forward, (mine, group)),
                (1.4 + group[-1] + skip, add_level, (0, mine, group)),
            ]
            if depth > 1:
                events += [(2.7 + group[-1] + skip, add_level, (1, mine, group))]
            for b in range(2, depth):
                now = 4.6 + 2 * group[-1] + (b - 2) * stride + (0 if mine else 1.4)
                events += [(now + 0.1, add_level, (b, mine, group))]
        for jj in range(parts):
            events += [(1.0 + jj + skip, receive_first, (mine, jj))]
            if depth > 1:
                events += [(2.3 + jj + skip, receive_total, (1, mine, jj))]
            for b in range(2, depth):
                now = 4.6 + 2 * jj + (b - 2) * stride + (0 if mine else 1.4)
                events += [(now, receive_total, (b, mine, jj))]
    for _, event, at in sorted(events, key=lambda item: item[0]):
        event(*at)

    squares = jnp.zeros((tokens, size), F32)
    crosses = jnp.zeros((tokens, size), F32)
    for mine, jj in chunk_list:
        for h in chunk_heads(mine, jj):
            z = readout[h] * scale_ref[h]
            readout[h] = z
            squares += z * z
            crosses += gain_ref[:, cols(h)] * dy_ref[:, cols(h)].astype(F32) * z

    stat_send[0:1, :] = jnp.sum(jnp.transpose(squares), axis=0, keepdims=True)
    stat_send[1:2, :] = jnp.sum(jnp.transpose(crosses), axis=0, keepdims=True)
    stat_copies = [
        remote(
            stat_send, stat_recv.at[d - 1], stat_ssem.at[d - 1], stat_rsem.at[d - 1],
            {"head": lax.rem(me + d, head_count)},
        )
        for d in range(1, head_count)
    ]
    for copy in stat_copies:
        copy.start()
    square_row = stat_send[0:1, :]
    cross_row = stat_send[1:2, :]
    for d, copy in enumerate(stat_copies):
        copy.wait_recv()
        square_row += stat_recv[d, 0:1, :]
        cross_row += stat_recv[d, 1:2, :]
    features = width * head_count
    rms = jnp.sqrt(square_row / features + EPSILON)
    coef = cross_row / (features * rms * rms * rms)
    inv_col[...] = jnp.transpose(jnp.broadcast_to(1.0 / rms, (size, tokens)))
    coef_col[...] = jnp.transpose(jnp.broadcast_to(coef, (size, tokens)))

    def message(b, h, flag=1.0):
        total = None
        for kind in range(kinds):
            term = (weight(kind, h, b + 1) * flag) * kind_sums[h, :, pl.ds(kind * size, size)]
            total = term if total is None else total + term
        return total

    def send_bucket_grad(mine, jj):
        for h in chunk_heads(mine, jj):
            back_send[1, h] = (grad_states[h] + message(1, h)).astype(BF16)
        back_copy(1, mine, jj).start()

    for mine, group in [(mine, group) for mine in (False, True) for group in groups]:
        for h in chunk_heads(mine, *group):
            gain = gain_ref[:, cols(h)]
            z = readout[h]
            att_ref[:, cols(h)] = (z * inv_col[...] * gain).astype(BF16)
            grad = gain * dy_ref[:, cols(h)].astype(F32) * inv_col[...] - z * coef_col[...]
            grad = (grad * scale_ref[h]).astype(BF16)
            grad_out_ref[h] = grad
            masked = jnp.concatenate(
                [jnp.where(kind_col[...] == kind, grad.astype(F32), 0.0).astype(BF16) for kind in range(kinds)],
                axis=1,
            )
            kind_sums[h] = dot(query_t[h], masked, NN)
            grad_states[h] = jnp.zeros((size, size), F32)
        if not mine:
            for b in reversed(range(2, depth)):

                @pl.when(upper[b])
                def _():
                    for jj in group:
                        for h in chunk_heads(mine, jj):
                            half_send[b, h] = message(b, h).astype(BF16)
                        half_copy(b, mine, jj).start()

        if depth > 1:

            @pl.when(jnp.logical_and(upper[1], jnp.logical_not(above[1])) if mine else upper[1])
            def _():
                for jj in group:
                    send_bucket_grad(mine, jj)

    stores = [
        pltpu.make_async_copy(src, dst, store_sem.at[i])
        for i, (src, dst) in enumerate(
            ((att_ref, att_hbm), (gq_ref, gq_hbm), (gk_ref, gk_hbm), (gv_ref, gv_hbm))
        )
    ]
    stores[0].start()

    def local_backward(mine, group):
        for h in chunk_heads(mine, *group):
            grad = grad_out_ref[h]
            scores = dot(grad, v_ref[:, cols(h)], NT)
            dprobs = (jnp.where(causal(), scores, 0.0) * token_weights(h, 0)).astype(BF16)
            key_acc[h] = dot(dprobs, q_ref[:, cols(h)], TN)
            value_acc[h] = dot(probs[h], grad, TN)
            readout[h] = dot(dprobs, k_ref[:, cols(h)], NN)
        for b in range(depth):

            @pl.when(upper[b])
            def _():
                for h in chunk_heads(mine, *group):
                    level = dot(grad_out_ref[h], fwd_recv[b, h], NT)
                    readout[h] += token_weights(h, b + 1) * level

        for h in chunk_heads(mine, *group):
            gq_ref[:, cols(h)] = readout[h].astype(BF16)

    def pass_half(b, jj):
        @pl.when(upper[b])
        def _():
            half_copy(b, True, jj).wait_recv()
            for h in chunk_heads(True, jj):
                total = grad_states[h] + message(b, h) + half_recv[b, h].astype(F32)
                back_send[b, h] = total.astype(BF16)
            back_copy(b, True, jj).start()

    def gather_grads(b, mine, jj):
        @pl.when(source[b])
        def _():
            for t in range(1 << (b - 1)):
                back_arrival(t, mine, jj).wait_recv()
                for h in chunk_heads(mine, jj):
                    grad_states[h] += back_recv[t, h].astype(F32)

    def pass_bucket_grad(jj):
        @pl.when(jnp.logical_and(upper[1], above[1]))
        def _():
            send_bucket_grad(True, jj)

    def send_last(mine, jj):
        @pl.when(takes(mine))
        def _():
            flag = side.astype(F32)
            for h in chunk_heads(mine, jj):
                last_send[h] = (grad_states[h] + message(0, h, flag)).astype(BF16)
            last_copy(mine, jj).start()

    def finish(mine, jj):
        @pl.when(gives(mine))
        def _():
            last_copy(mine, jj).wait_recv()
            for h in chunk_heads(mine, jj):
                grad_states[h] += last_recv[h].astype(F32)

        for h in chunk_heads(mine, jj):
            state = grad_states[h].astype(BF16)
            gk_ref[:, cols(h)] = (key_acc[h] + dot(v_ref[:, cols(h)], state, NT)).astype(BF16)
            gv_ref[:, cols(h)] = (value_acc[h] + dot(k_ref[:, cols(h)], state, NN)).astype(BF16)

    events = []
    late = max(depth - 3, 0) * stride
    for group in groups:
        events += [
            (0.9 + 0.2 * group[0], local_backward, (False, group)),
            (2.3 + 0.2 * group[0], local_backward, (True, group)),
        ]
    for jj in range(parts):
        for b in range(2, depth):
            now = (depth - 1 - b) * stride
            events += [
                (now + 1.0 + jj, pass_half, (b, jj)),
                (now + 3.3 + 2 * jj, gather_grads, (b, True, jj)),
            ]
        if depth > 1:
            events += [
                (late + 3.4 + 2 * jj, pass_bucket_grad, (jj,)),
                (late + 2.5 + jj, gather_grads, (1, False, jj)),
                (late + 4.7 + 2 * jj, gather_grads, (1, True, jj)),
            ]
        events += [
            (late + 2.6 + jj, send_last, (False, jj)),
            (late + 4.8 + 2 * jj, send_last, (True, jj)),
            (late + 5.0 + 2 * jj, finish, (True, jj)),
            (late + 5.9 + 2 * jj, finish, (False, jj)),
        ]
    for _, event, at in sorted(events, key=lambda item: item[0]):
        event(*at)
    for store in stores[1:]:
        store.start()

    for copy in stat_copies:
        copy.wait_send()
    for mine, jj in chunk_list:

        @pl.when(gives(mine))
        def _():
            own_copy(mine, jj).wait_send()

        @pl.when(takes(mine))
        def _():
            last_copy(mine, jj).wait_send()

        for b in range(1, depth):
            if mine or b == 1:

                @pl.when(source[b])
                def _():
                    for t in range(1 << (b - 1)):
                        total_copy(b, t, mine, jj).wait_send()

                @pl.when(upper[b])
                def _():
                    back_copy(b, mine, jj).wait_send()
                    if b > 1:
                        relay_copy(b, mine, jj).wait_send()

            else:

                @pl.when(upper[b])
                def _():
                    half_copy(b, mine, jj).wait_send()

    for store in stores:
        store.wait()


def land(*refs):
    count = len(refs) // 2
    for source, target in zip(refs[:count], refs[count:]):
        target[...] = source[...]


def solution(mesh):
    ctx_count, head_count = mesh.shape["ctx"], mesh.shape["head"]
    depth = ctx_count.bit_length() - 1
    targets = max(ctx_count // 4, 1)

    def shards(queries, keys, values, grad_out, token_kind, level_table, head_scale, norm_gain):
        tokens, width = queries.shape
        kinds, heads, _ = level_table.shape
        size = width // heads
        chunks = heads // CHUNK
        hbm = pl.BlockSpec(memory_space=pltpu.HBM)
        block = jax.ShapeDtypeStruct((tokens, width), BF16)
        square = (heads, size, size)
        dma = pltpu.SemaphoreType.DMA
        results = pl.pallas_call(
            functools.partial(kernel, ctx_count, head_count),
            out_shape=(block,) * 4,
            in_specs=[hbm] * 8,
            out_specs=(hbm,) * 4,
            scratch_shapes=[pltpu.VMEM((tokens, width), BF16)] * 4
            + [
                pltpu.VMEM((1, tokens), jnp.int32),
                pltpu.SMEM(level_table.shape, jnp.int32),
                pltpu.SMEM((heads,), F32),
                pltpu.VMEM((1, width), F32),
            ]
            + [pltpu.VMEM((tokens, width), BF16)] * 4
            + [pltpu.VMEM((tokens, size), F32)] * 3
            + [
                pltpu.VMEM(square, F32),
                pltpu.VMEM((heads, tokens, tokens), BF16),
                pltpu.VMEM((heads, size, tokens), BF16),
                pltpu.VMEM((heads, tokens, size), F32),
                pltpu.VMEM((heads, tokens, size), BF16),
                pltpu.VMEM((heads, size, kinds * size), F32),
                pltpu.VMEM(square, F32),
                pltpu.VMEM((heads, tokens, size), F32),
                pltpu.VMEM((heads, tokens, size), F32),
                pltpu.VMEM(square, BF16),
                pltpu.VMEM(square, BF16),
                pltpu.VMEM((depth,) + square, BF16),
                pltpu.VMEM((depth,) + square, BF16),
                pltpu.VMEM((depth,) + square, BF16),
                pltpu.VMEM((depth,) + square, BF16),
                pltpu.VMEM((targets,) + square, BF16),
                pltpu.VMEM(square, BF16),
                pltpu.VMEM(square, BF16),
                pltpu.VMEM((8, tokens), F32),
                pltpu.VMEM((head_count - 1, 8, tokens), F32),
                dma((8,)),
                dma((4,)),
                dma((chunks,)),
                dma((targets, chunks)),
                dma((depth, chunks)),
                dma((depth, chunks)),
                dma((depth, chunks)),
                dma((depth, chunks)),
                dma((depth, chunks)),
                dma((targets, chunks)),
                dma((chunks,)),
                dma((chunks,)),
                dma((head_count - 1,)),
                dma((head_count - 1,)),
            ],
            compiler_params=pltpu.CompilerParams(
                collective_id=0, has_side_effects=True, vmem_limit_bytes=64 * 1024 * 1024
            ),
            cost_estimate=pl.CostEstimate(
                flops=36 * heads * tokens * size * size, bytes_accessed=16 * tokens * width, transcendentals=0
            ),
        )(
            queries, keys, values, grad_out,
            token_kind.reshape(1, tokens), level_table, head_scale, norm_gain.reshape(1, width),
        )
        rows = pl.BlockSpec((tokens // 2, width), lambda i: (i, 0))
        return pl.pallas_call(
            land,
            out_shape=(block,) * 4,
            grid=(2,),
            in_specs=[rows] * 4,
            out_specs=(rows,) * 4,
            compiler_params=pltpu.CompilerParams(vmem_limit_bytes=64 * 1024 * 1024),
        )(*results)

    in_specs = (
        P("ctx", "head"),
        P("ctx", "head"),
        P("ctx", "head"),
        P("ctx", "head"),
        P("ctx"),
        P(None, "head", None),
        P("head"),
        P("head"),
    )
    return jax.shard_map(
        shards, mesh=mesh, in_specs=in_specs, out_specs=(P("ctx", "head"),) * 4, check_vma=False
    )
```

```python
import functools

import jax
import jax.numpy as jnp
from jax import lax
from jax.experimental import pallas as pl
from jax.experimental.pallas import tpu as pltpu
from jax.sharding import PartitionSpec as P

EPSILON = 1e-06
CHUNK = 4
GROUP = 1
F32 = jnp.float32
BF16 = jnp.bfloat16


def factor(level):
    return 0.25 * 2.0 ** (-0.5 * level)


def dot(left, right, contract):
    return lax.dot_general(left, right, (contract, ((), ())), preferred_element_type=F32)


NN = ((1,), (0,))
NT = ((1,), (1,))
TN = ((0,), (0,))


def kernel(
    ctx_count, head_count,
    q_hbm, k_hbm, v_hbm, dy_hbm, kind_hbm, table_hbm, scale_hbm, gain_hbm,
    att_hbm, gq_hbm, gk_hbm, gv_hbm,
    q_ref, k_ref, v_ref, dy_ref, kind_ref, table_ref, scale_ref, gain_ref,
    att_ref, gq_ref, gk_ref, gv_ref, kind_col, inv_col, coef_col,
    states, probs, query_t, readout, grad_out_ref, kind_sums, grad_states, key_acc, value_acc,
    own_send, total_send, fwd_recv, half_send, half_recv, back_send, back_recv, last_send, last_recv, late_send, late_recv,
    stat_send, stat_recv,
    load_sem, store_sem, own_ssem, total_ssem, relay_ssem, fwd_rsem, half_ssem, half_rsem,
    back_ssem, back_rsem, last_ssem, last_rsem, late_ssem, late_rsem, stat_ssem, stat_rsem,
):
    tokens, width = q_ref.shape
    heads, size, _ = states.shape
    kinds = table_ref.shape[0]
    depth = ctx_count.bit_length() - 1
    pairs = ctx_count // 2
    half = heads // 2
    parts = half // CHUNK
    c = lax.axis_index("ctx")
    me = lax.axis_index("head")
    pair, side = c >> 1, c & 1
    mesh_id = pl.DeviceIdType.MESH
    odd = side == 1
    inner = pair != pairs - 1
    upper = [((c >> b) & 1) == 1 for b in range(depth)]
    source = [None] + [(pair & ((1 << b) - 1)) == (1 << (b - 1)) - 1 for b in range(1, depth)]
    above = [None] + [
        jnp.logical_and(inner, (pair & ((1 << b) - 1)) == (1 << b) - 1) for b in range(1, depth)
    ]
    place = [None] + [pair & ((1 << (b - 1)) - 1) for b in range(1, depth)]
    origin = [None] + [pair - place[b] - 1 for b in range(1, depth)]
    beside = {"ctx": c ^ 1}
    if depth > 1:
        late_gives = above[1]
        late_takes = jnp.logical_and(source[1], pair + 1 != pairs - 1)

    def at_pair(other):
        return {"ctx": 2 * other + side}

    loads = [
        pltpu.make_async_copy(src, dst, load_sem.at[i])
        for i, (src, dst) in enumerate(
            (
                (k_hbm, k_ref), (v_hbm, v_ref), (q_hbm, q_ref), (dy_hbm, dy_ref),
                (kind_hbm, kind_ref), (table_hbm, table_ref), (scale_hbm, scale_ref), (gain_hbm, gain_ref),
            )
        )
    ]
    for load in loads:
        load.start()

    barrier = pltpu.get_barrier_semaphore()

    def greet(device):
        pl.semaphore_signal(barrier, inc=1, device_id=device, device_id_type=mesh_id)

    greet(beside)
    for d in range(1, head_count):
        greet({"head": lax.rem(me + d, head_count)})
    greeted = head_count
    for b in range(1, depth):

        @pl.when(upper[b])
        def _():
            greet(at_pair(origin[b]))

        @pl.when(source[b])
        def _():
            for t in range(1 << (b - 1)):
                greet(at_pair(pair + 1 + t))

        if b == 1:

            @pl.when(late_gives)
            def _():
                greet({"ctx": (c - 2) ^ 1})

            @pl.when(late_takes)
            def _():
                greet({"ctx": (c + 2) ^ 1})

            greeted = greeted + jnp.where(jnp.logical_or(late_gives, late_takes), 1, 0)
        greeted = greeted + ((c >> b) & 1) + jnp.where(source[b], 1 << (b - 1), 0)

    def first_chunk(mine, jj):
        return (side if mine else 1 - side) * parts + jj

    def chunk_heads(mine, *several):
        return [first_chunk(mine, jj) * CHUNK + i for jj in several for i in range(CHUNK)]

    def part(mine, jj):
        return pl.ds(first_chunk(mine, jj) * CHUNK, CHUNK)

    def cols(h):
        return pl.ds(pl.multiple_of(h * size, size), size)

    def remote(src, dst, ssem, rsem, device):
        return pltpu.make_async_remote_copy(
            src_ref=src, dst_ref=dst, send_sem=ssem, recv_sem=rsem, device_id=device, device_id_type=mesh_id
        )

    def own_copy(mine, jj):
        at, j = part(mine, jj), first_chunk(mine, jj)
        return remote(own_send.at[at], fwd_recv.at[0, at], own_ssem.at[j], fwd_rsem.at[0, j], beside)

    def total_copy(b, t, mine, jj):
        at, j = part(mine, jj), first_chunk(mine, jj)
        return remote(
            total_send.at[at], fwd_recv.at[b, at], total_ssem.at[t, j], fwd_rsem.at[b, j], at_pair(pair + 1 + t)
        )

    def relay_copy(b, mine, jj):
        at, j = part(mine, jj), first_chunk(mine, jj)
        return remote(fwd_recv.at[b, at], fwd_recv.at[b, at], relay_ssem.at[b, j], fwd_rsem.at[b, j], beside)

    def half_copy(b, mine, jj):
        at, j = part(mine, jj), first_chunk(mine, jj)
        return remote(half_send.at[b, at], half_recv.at[b, at], half_ssem.at[b, j], half_rsem.at[b, j], beside)

    def back_copy(b, mine, jj):
        at, j = part(mine, jj), first_chunk(mine, jj)
        return remote(
            back_send.at[b, at], back_recv.at[place[b], at], back_ssem.at[b, j], back_rsem.at[place[b], j],
            at_pair(origin[b]),
        )

    def back_arrival(t, mine, jj):
        at, j = part(mine, jj), first_chunk(mine, jj)
        return remote(back_send.at[0, at], back_recv.at[t, at], back_ssem.at[0, j], back_rsem.at[t, j], beside)

    def last_copy(mine, jj):
        at, j = part(mine, jj), first_chunk(mine, jj)
        return remote(last_send.at[at], last_recv.at[at], last_ssem.at[j], last_rsem.at[j], beside)

    def late_copy(across, jj):
        at, j = part(True, jj), first_chunk(True, jj)
        device = {"ctx": (c - 2) ^ 1} if across else {"ctx": c - 2}
        return remote(late_send.at[at], late_recv.at[at], late_ssem.at[int(across), j], late_rsem.at[j], device)

    def late_arrival(mine, jj):
        at, j = part(mine, jj), first_chunk(mine, jj)
        return remote(late_send.at[at], late_recv.at[at], late_ssem.at[0, j], late_rsem.at[j], beside)

    def takes(mine):
        return jnp.logical_or(odd, jnp.logical_and(inner, True if mine else source[1]))

    def gives(mine):
        return jnp.logical_or(side == 0, jnp.logical_and(inner, source[1] if mine else True))

    chunk_list = [(mine, jj) for mine in (False, True) for jj in range(parts)]
    groups = [tuple(range(jj, min(jj + GROUP, parts))) for jj in range(0, parts, GROUP)]

    def weight(kind, h, level):
        return table_ref[kind, h, level].astype(F32) * factor(level)

    def token_weights(h, level):
        out = jnp.full((tokens, size), weight(0, h, level), F32)
        for kind in range(1, kinds):
            out = jnp.where(kind_col[...] == kind, weight(kind, h, level), out)
        return out

    def causal():
        row = lax.broadcasted_iota(jnp.int32, (tokens, tokens), 0)
        col = lax.broadcasted_iota(jnp.int32, (tokens, tokens), 1)
        return col <= row

    loads[0].wait()
    loads[1].wait()
    for index, (mine, jj) in enumerate(chunk_list):
        for h in chunk_heads(mine, jj):
            state = dot(k_ref[:, cols(h)], v_ref[:, cols(h)], TN)
            states[h] = state
            own_send[h] = state.astype(BF16)
        if index == 0:
            pl.semaphore_wait(barrier, greeted)

        @pl.when(gives(mine))
        def _():
            own_copy(mine, jj).start()

    for load in loads[2:]:
        load.wait()
    kind_col[...] = jnp.transpose(
        jnp.broadcast_to(kind_ref[...].astype(F32), (size, tokens))
    )

    def local_forward(mine, group):
        for h in chunk_heads(mine, *group):
            q = q_ref[:, cols(h)]
            scores = dot(q, k_ref[:, cols(h)], NT)
            attn = (jnp.where(causal(), scores, 0.0) * token_weights(h, 0)).astype(BF16)
            probs[h] = attn
            readout[h] = dot(attn, v_ref[:, cols(h)], NN)
            query_t[h] = jnp.transpose(q)

    def send_total(b, mine, jj):
        for h in chunk_heads(mine, jj):
            total_send[h] = states[h].astype(BF16)
        for t in reversed(range(1 << (b - 1))):
            total_copy(b, t, mine, jj).start()

    def add_level(b, mine, group):
        @pl.when(upper[b])
        def _():
            for h in chunk_heads(mine, *group):
                level = dot(q_ref[:, cols(h)], fwd_recv[b, h], NN)
                readout[h] += token_weights(h, b + 1) * level

    def add_state(b, mine, jj):
        for h in chunk_heads(mine, jj):
            states[h] += fwd_recv[b, h].astype(F32)

    def receive_first(mine, jj):
        @pl.when(takes(mine))
        def _():
            own_copy(mine, jj).wait_recv()
            add_state(0, mine, jj)

        if depth > 1:

            @pl.when(source[1])
            def _():
                send_total(1, mine, jj)

    def receive_total(b, mine, jj):
        @pl.when(upper[b])
        def _():
            total_copy(b, 0, mine, jj).wait_recv()
            if b > 1 and mine:
                relay_copy(b, mine, jj).start()

        if mine and b + 1 < depth:

            @pl.when(above[b])
            def _():
                add_state(b, mine, jj)

            @pl.when(source[b + 1])
            def _():
                send_total(b + 1, mine, jj)

    events = []
    stride = 3 * parts + 5
    for mine in (True, False):
        skip = 0 if mine else parts
        for group in groups:
            events += [
                (0.5 + group[0] + skip, local_forward, (mine, group)),
                (1.4 + group[-1] + skip, add_level, (0, mine, group)),
            ]
            if depth > 1:
                events += [(2.7 + group[-1] + skip, add_level, (1, mine, group))]
            for b in range(2, depth):
                now = 4.6 + 2 * group[-1] + (b - 2) * stride + (0 if mine else 1.4)
                events += [(now + 0.1, add_level, (b, mine, group))]
        for jj in range(parts):
            events += [(1.0 + jj + skip, receive_first, (mine, jj))]
            if depth > 1:
                events += [(2.3 + jj + skip, receive_total, (1, mine, jj))]
            for b in range(2, depth):
                now = 4.6 + 2 * jj + (b - 2) * stride + (0 if mine else 1.4)
                events += [(now, receive_total, (b, mine, jj))]
    for _, event, at in sorted(events, key=lambda item: item[0]):
        event(*at)

    squares = jnp.zeros((tokens, size), F32)
    crosses = jnp.zeros((tokens, size), F32)
    for mine, jj in chunk_list:
        for h in chunk_heads(mine, jj):
            z = readout[h] * scale_ref[h]
            readout[h] = z
            squares += z * z
            crosses += gain_ref[:, cols(h)] * dy_ref[:, cols(h)].astype(F32) * z

    stat_send[0:1, :] = jnp.sum(jnp.transpose(squares), axis=0, keepdims=True)
    stat_send[1:2, :] = jnp.sum(jnp.transpose(crosses), axis=0, keepdims=True)
    stat_copies = [
        remote(
            stat_send, stat_recv.at[d - 1], stat_ssem.at[d - 1], stat_rsem.at[d - 1],
            {"head": lax.rem(me + d, head_count)},
        )
        for d in range(1, head_count)
    ]
    for copy in stat_copies:
        copy.start()
    square_row = stat_send[0:1, :]
    cross_row = stat_send[1:2, :]
    for d, copy in enumerate(stat_copies):
        copy.wait_recv()
        square_row += stat_recv[d, 0:1, :]
        cross_row += stat_recv[d, 1:2, :]
    features = width * head_count
    rms = jnp.sqrt(square_row / features + EPSILON)
    coef = cross_row / (features * rms * rms * rms)
    inv_col[...] = jnp.transpose(jnp.broadcast_to(1.0 / rms, (size, tokens)))
    coef_col[...] = jnp.transpose(jnp.broadcast_to(coef, (size, tokens)))

    def message(b, h, flag=1.0):
        total = None
        for kind in range(kinds):
            term = (weight(kind, h, b + 1) * flag) * kind_sums[h, :, pl.ds(kind * size, size)]
            total = term if total is None else total + term
        return total

    def send_bucket_grad(mine, jj):
        for h in chunk_heads(mine, jj):
            back_send[1, h] = message(1, h).astype(BF16)
        back_copy(1, mine, jj).start()

    for mine, group in [(mine, group) for mine in (False, True) for group in groups]:
        for h in chunk_heads(mine, *group):
            gain = gain_ref[:, cols(h)]
            z = readout[h]
            att_ref[:, cols(h)] = (z * inv_col[...] * gain).astype(BF16)
            grad = gain * dy_ref[:, cols(h)].astype(F32) * inv_col[...] - z * coef_col[...]
            grad = (grad * scale_ref[h]).astype(BF16)
            grad_out_ref[h] = grad
            masked = jnp.concatenate(
                [jnp.where(kind_col[...] == kind, grad.astype(F32), 0.0).astype(BF16) for kind in range(kinds)],
                axis=1,
            )
            kind_sums[h] = dot(query_t[h], masked, NN)
            grad_states[h] = jnp.zeros((size, size), F32)
        if not mine:
            for b in reversed(range(2, depth)):

                @pl.when(upper[b])
                def _():
                    for jj in group:
                        for h in chunk_heads(mine, jj):
                            half_send[b, h] = message(b, h).astype(BF16)
                        half_copy(b, mine, jj).start()

        if depth > 1:

            @pl.when(upper[1])
            def _():
                for jj in group:
                    send_bucket_grad(mine, jj)

    stores = [
        pltpu.make_async_copy(src, dst, store_sem.at[i])
        for i, (src, dst) in enumerate(
            ((att_ref, att_hbm), (gq_ref, gq_hbm), (gk_ref, gk_hbm), (gv_ref, gv_hbm))
        )
    ]
    stores[0].start()

    def local_backward(mine, group):
        for h in chunk_heads(mine, *group):
            grad = grad_out_ref[h]
            scores = dot(grad, v_ref[:, cols(h)], NT)
            dprobs = (jnp.where(causal(), scores, 0.0) * token_weights(h, 0)).astype(BF16)
            key_acc[h] = dot(dprobs, q_ref[:, cols(h)], TN)
            value_acc[h] = dot(probs[h], grad, TN)
            readout[h] = dot(dprobs, k_ref[:, cols(h)], NN)
        for b in range(depth):

            @pl.when(upper[b])
            def _():
                for h in chunk_heads(mine, *group):
                    level = dot(grad_out_ref[h], fwd_recv[b, h], NT)
                    readout[h] += token_weights(h, b + 1) * level

        for h in chunk_heads(mine, *group):
            gq_ref[:, cols(h)] = readout[h].astype(BF16)

    def pass_half(b, jj):
        @pl.when(upper[b])
        def _():
            half_copy(b, True, jj).wait_recv()
            for h in chunk_heads(True, jj):
                total = grad_states[h] + message(b, h) + half_recv[b, h].astype(F32)
                back_send[b, h] = total.astype(BF16)
            back_copy(b, True, jj).start()

    def gather_grads(b, mine, jj):
        @pl.when(source[b])
        def _():
            for t in range(1 << (b - 1)):
                back_arrival(t, mine, jj).wait_recv()
                for h in chunk_heads(mine, jj):
                    grad_states[h] += back_recv[t, h].astype(F32)

    def send_late(jj):
        @pl.when(late_gives)
        def _():
            for h in chunk_heads(True, jj):
                late_send[h] = grad_states[h].astype(BF16)
            for across in (True, False):
                late_copy(across, jj).start()

    def receive_late(mine, jj):
        @pl.when(late_takes)
        def _():
            late_arrival(mine, jj).wait_recv()
            for h in chunk_heads(mine, jj):
                grad_states[h] += late_recv[h].astype(F32)

    def send_last(mine, jj, when):
        @pl.when(jnp.logical_and(takes(mine), when))
        def _():
            flag = side.astype(F32)
            for h in chunk_heads(mine, jj):
                last_send[h] = (grad_states[h] + message(0, h, flag)).astype(BF16)
            last_copy(mine, jj).start()

    def finish(mine, jj):
        @pl.when(gives(mine))
        def _():
            last_copy(mine, jj).wait_recv()
            for h in chunk_heads(mine, jj):
                grad_states[h] += last_recv[h].astype(F32)

        for h in chunk_heads(mine, jj):
            state = grad_states[h].astype(BF16)
            gk_ref[:, cols(h)] = (key_acc[h] + dot(v_ref[:, cols(h)], state, NT)).astype(BF16)
            gv_ref[:, cols(h)] = (value_acc[h] + dot(k_ref[:, cols(h)], state, NN)).astype(BF16)

    def store_queries():
        stores[1].start()

    events = [(2.49, store_queries, ())]
    late = max(depth - 3, 0) * stride
    for group in groups:
        events += [
            (0.9 + 0.2 * group[0], local_backward, (False, group)),
            (2.3 + 0.2 * group[0], local_backward, (True, group)),
        ]
    for jj in range(parts):
        for b in range(2, depth):
            now = (depth - 1 - b) * stride
            events += [
                (now + 1.0 + jj, pass_half, (b, jj)),
                (now + 3.3 + 2 * jj, gather_grads, (b, True, jj)),
            ]
        if depth > 1:
            events += [
                (late + 2.5 + 0.01 * jj, gather_grads, (1, False, jj)),
                (late + 2.7 + 0.01 * jj, gather_grads, (1, True, jj)),
                (late + 3.4 + 2 * jj, send_late, (jj,)),
                (late + 3.5 + 2 * jj, send_last, (True, jj, late_gives)),
                (late + 5.0 + 2 * jj, receive_late, (True, jj)),
                (late + 5.2 + 2 * jj, receive_late, (False, jj)),
            ]
        events += [
            (late + 2.6 + 0.01 * jj, send_last, (False, jj, True)),
            (late + 2.8 + 0.01 * jj, send_last, (True, jj, jnp.logical_not(late_gives) if depth > 1 else True)),
            (late + 5.1 + 2 * jj, finish, (True, jj)),
            (late + 5.3 + 2 * jj, finish, (False, jj)),
        ]
    for _, event, at in sorted(events, key=lambda item: item[0]):
        event(*at)
    for store in stores[2:]:
        store.start()

    for copy in stat_copies:
        copy.wait_send()
    for mine, jj in chunk_list:

        @pl.when(gives(mine))
        def _():
            own_copy(mine, jj).wait_send()

        if mine and depth > 1:

            @pl.when(late_gives)
            def _():
                for across in (True, False):
                    late_copy(across, jj).wait_send()

        @pl.when(takes(mine))
        def _():
            last_copy(mine, jj).wait_send()

        for b in range(1, depth):
            if mine or b == 1:

                @pl.when(source[b])
                def _():
                    for t in range(1 << (b - 1)):
                        total_copy(b, t, mine, jj).wait_send()

                @pl.when(upper[b])
                def _():
                    back_copy(b, mine, jj).wait_send()
                    if b > 1:
                        relay_copy(b, mine, jj).wait_send()

            else:

                @pl.when(upper[b])
                def _():
                    half_copy(b, mine, jj).wait_send()

    for store in stores:
        store.wait()


def land(*refs):
    count = len(refs) // 2
    for source, target in zip(refs[:count], refs[count:]):
        target[...] = source[...]


def solution(mesh):
    ctx_count, head_count = mesh.shape["ctx"], mesh.shape["head"]
    depth = ctx_count.bit_length() - 1
    targets = max(ctx_count // 4, 1)

    def shards(queries, keys, values, grad_out, token_kind, level_table, head_scale, norm_gain):
        tokens, width = queries.shape
        kinds, heads, _ = level_table.shape
        size = width // heads
        chunks = heads // CHUNK
        hbm = pl.BlockSpec(memory_space=pltpu.HBM)
        block = jax.ShapeDtypeStruct((tokens, width), BF16)
        square = (heads, size, size)
        dma = pltpu.SemaphoreType.DMA
        results = pl.pallas_call(
            functools.partial(kernel, ctx_count, head_count),
            out_shape=(block,) * 4,
            in_specs=[hbm] * 8,
            out_specs=(hbm,) * 4,
            scratch_shapes=[pltpu.VMEM((tokens, width), BF16)] * 4
            + [
                pltpu.VMEM((1, tokens), jnp.int32),
                pltpu.SMEM(level_table.shape, jnp.int32),
                pltpu.SMEM((heads,), F32),
                pltpu.VMEM((1, width), F32),
            ]
            + [pltpu.VMEM((tokens, width), BF16)] * 4
            + [pltpu.VMEM((tokens, size), F32)] * 3
            + [
                pltpu.VMEM(square, F32),
                pltpu.VMEM((heads, tokens, tokens), BF16),
                pltpu.VMEM((heads, size, tokens), BF16),
                pltpu.VMEM((heads, tokens, size), F32),
                pltpu.VMEM((heads, tokens, size), BF16),
                pltpu.VMEM((heads, size, kinds * size), F32),
                pltpu.VMEM(square, F32),
                pltpu.VMEM((heads, tokens, size), F32),
                pltpu.VMEM((heads, tokens, size), F32),
                pltpu.VMEM(square, BF16),
                pltpu.VMEM(square, BF16),
                pltpu.VMEM((depth,) + square, BF16),
                pltpu.VMEM((depth,) + square, BF16),
                pltpu.VMEM((depth,) + square, BF16),
                pltpu.VMEM((depth,) + square, BF16),
                pltpu.VMEM((targets,) + square, BF16),
                pltpu.VMEM(square, BF16),
                pltpu.VMEM(square, BF16),
                pltpu.VMEM(square, BF16),
                pltpu.VMEM(square, BF16),
                pltpu.VMEM((8, tokens), F32),
                pltpu.VMEM((head_count - 1, 8, tokens), F32),
                dma((8,)),
                dma((4,)),
                dma((chunks,)),
                dma((targets, chunks)),
                dma((depth, chunks)),
                dma((depth, chunks)),
                dma((depth, chunks)),
                dma((depth, chunks)),
                dma((depth, chunks)),
                dma((targets, chunks)),
                dma((chunks,)),
                dma((chunks,)),
                dma((2, chunks)),
                dma((chunks,)),
                dma((head_count - 1,)),
                dma((head_count - 1,)),
            ],
            compiler_params=pltpu.CompilerParams(
                collective_id=0, has_side_effects=True, vmem_limit_bytes=64 * 1024 * 1024
            ),
            cost_estimate=pl.CostEstimate(
                flops=36 * heads * tokens * size * size, bytes_accessed=16 * tokens * width, transcendentals=0
            ),
        )(
            queries, keys, values, grad_out,
            token_kind.reshape(1, tokens), level_table, head_scale, norm_gain.reshape(1, width),
        )
        rows = pl.BlockSpec((tokens // 2, width), lambda i: (i, 0))
        return pl.pallas_call(
            land,
            out_shape=(block,) * 4,
            grid=(2,),
            in_specs=[rows] * 4,
            out_specs=(rows,) * 4,
            compiler_params=pltpu.CompilerParams(vmem_limit_bytes=64 * 1024 * 1024),
        )(*results)

    in_specs = (
        P("ctx", "head"),
        P("ctx", "head"),
        P("ctx", "head"),
        P("ctx", "head"),
        P("ctx"),
        P(None, "head", None),
        P("head"),
        P("head"),
    )
    return jax.shard_map(
        shards, mesh=mesh, in_specs=in_specs, out_specs=(P("ctx", "head"),) * 4, check_vma=False
    )
```

```python
import functools

import jax
import jax.numpy as jnp
from jax import lax
from jax.experimental import pallas as pl
from jax.experimental.pallas import tpu as pltpu
from jax.sharding import PartitionSpec as P

EPSILON = 1e-06
CHUNK = 4
GROUP = 1
AHEAD = 2
F32 = jnp.float32
BF16 = jnp.bfloat16


def factor(level):
    return 0.25 * 2.0 ** (-0.5 * level)


def dot(left, right, contract):
    return lax.dot_general(left, right, (contract, ((), ())), preferred_element_type=F32)


NN = ((1,), (0,))
NT = ((1,), (1,))
TN = ((0,), (0,))


def kernel(
    ctx_count, head_count,
    q_hbm, k_hbm, v_hbm, dy_hbm, kind_hbm, table_hbm, scale_hbm, gain_hbm,
    att_hbm, gq_hbm, gk_hbm, gv_hbm,
    q_ref, k_ref, v_ref, dy_ref, kind_ref, table_ref, scale_ref, gain_ref,
    att_ref, gq_ref, gk_ref, gv_ref, kind_col, inv_col, coef_col,
    states, probs, query_t, readout, grad_out_ref, kind_sums, grad_states, key_acc, value_acc,
    own_send, total_send, fwd_recv, half_send, half_recv, back_send, back_recv, last_send, last_recv, late_send, late_recv,
    stat_send, stat_recv,
    load_sem, store_sem, own_ssem, total_ssem, relay_ssem, fwd_rsem, half_ssem, half_rsem,
    back_ssem, back_rsem, last_ssem, last_rsem, late_ssem, late_rsem, stat_ssem, stat_rsem,
):
    tokens, width = q_ref.shape
    heads, size, _ = states.shape
    kinds = table_ref.shape[0]
    depth = ctx_count.bit_length() - 1
    pairs = ctx_count // 2
    half = heads // 2
    parts = half // CHUNK
    ahead_parts = half // AHEAD
    c = lax.axis_index("ctx")
    me = lax.axis_index("head")
    pair, side = c >> 1, c & 1
    mesh_id = pl.DeviceIdType.MESH
    odd = side == 1
    inner = pair != pairs - 1
    upper = [((c >> b) & 1) == 1 for b in range(depth)]
    source = [None] + [(pair & ((1 << b) - 1)) == (1 << (b - 1)) - 1 for b in range(1, depth)]
    above = [None] + [
        jnp.logical_and(inner, (pair & ((1 << b) - 1)) == (1 << b) - 1) for b in range(1, depth)
    ]
    place = [None] + [pair & ((1 << (b - 1)) - 1) for b in range(1, depth)]
    origin = [None] + [pair - place[b] - 1 for b in range(1, depth)]
    beside = {"ctx": c ^ 1}
    if depth > 1:
        late_gives = above[1]
        late_takes = jnp.logical_and(source[1], pair + 1 != pairs - 1)

    def at_pair(other):
        return {"ctx": 2 * other + side}

    loads = [
        pltpu.make_async_copy(src, dst, load_sem.at[i])
        for i, (src, dst) in enumerate(
            (
                (k_hbm, k_ref), (v_hbm, v_ref), (q_hbm, q_ref), (dy_hbm, dy_ref),
                (kind_hbm, kind_ref), (table_hbm, table_ref), (scale_hbm, scale_ref), (gain_hbm, gain_ref),
            )
        )
    ]
    for load in loads:
        load.start()

    barrier = pltpu.get_barrier_semaphore()

    def greet(device):
        pl.semaphore_signal(barrier, inc=1, device_id=device, device_id_type=mesh_id)

    greet(beside)
    for d in range(1, head_count):
        greet({"head": lax.rem(me + d, head_count)})
    greeted = head_count
    for b in range(1, depth):

        @pl.when(upper[b])
        def _():
            greet(at_pair(origin[b]))

        @pl.when(source[b])
        def _():
            for t in range(1 << (b - 1)):
                greet(at_pair(pair + 1 + t))

        if b == 1:

            @pl.when(late_gives)
            def _():
                greet({"ctx": (c - 2) ^ 1})

            @pl.when(late_takes)
            def _():
                greet({"ctx": (c + 2) ^ 1})

            greeted = greeted + jnp.where(jnp.logical_or(late_gives, late_takes), 1, 0)
        greeted = greeted + ((c >> b) & 1) + jnp.where(source[b], 1 << (b - 1), 0)

    def first_chunk(mine, jj, count=CHUNK):
        return (side if mine else 1 - side) * (half // count) + jj

    def chunk_heads(mine, *several, count=CHUNK):
        return [first_chunk(mine, jj, count) * count + i for jj in several for i in range(count)]

    def part(mine, jj, count=CHUNK):
        return pl.ds(first_chunk(mine, jj, count) * count, count)

    def cols(h):
        return pl.ds(pl.multiple_of(h * size, size), size)

    def remote(src, dst, ssem, rsem, device):
        return pltpu.make_async_remote_copy(
            src_ref=src, dst_ref=dst, send_sem=ssem, recv_sem=rsem, device_id=device, device_id_type=mesh_id
        )

    def own_copy(mine, jj):
        at, j = part(mine, jj, AHEAD), first_chunk(mine, jj, AHEAD)
        return remote(own_send.at[at], fwd_recv.at[0, at], own_ssem.at[j], fwd_rsem.at[0, j], beside)

    def total_copy(b, t, mine, jj):
        at, j = part(mine, jj, AHEAD), first_chunk(mine, jj, AHEAD)
        return remote(
            total_send.at[at], fwd_recv.at[b, at], total_ssem.at[t, j], fwd_rsem.at[b, j], at_pair(pair + 1 + t)
        )

    def relay_copy(b, mine, jj):
        at, j = part(mine, jj, AHEAD), first_chunk(mine, jj, AHEAD)
        return remote(fwd_recv.at[b, at], fwd_recv.at[b, at], relay_ssem.at[b, j], fwd_rsem.at[b, j], beside)

    def half_copy(b, mine, jj):
        at, j = part(mine, jj), first_chunk(mine, jj)
        return remote(half_send.at[b, at], half_recv.at[b, at], half_ssem.at[b, j], half_rsem.at[b, j], beside)

    def back_copy(b, mine, jj):
        at, j = part(mine, jj), first_chunk(mine, jj)
        return remote(
            back_send.at[b, at], back_recv.at[place[b], at], back_ssem.at[b, j], back_rsem.at[place[b], j],
            at_pair(origin[b]),
        )

    def back_arrival(t, mine, jj):
        at, j = part(mine, jj), first_chunk(mine, jj)
        return remote(back_send.at[0, at], back_recv.at[t, at], back_ssem.at[0, j], back_rsem.at[t, j], beside)

    def last_copy(mine, jj):
        at, j = part(mine, jj), first_chunk(mine, jj)
        return remote(last_send.at[at], last_recv.at[at], last_ssem.at[j], last_rsem.at[j], beside)

    def late_copy(across, jj):
        at, j = part(True, jj), first_chunk(True, jj)
        device = {"ctx": (c - 2) ^ 1} if across else {"ctx": c - 2}
        return remote(late_send.at[at], late_recv.at[at], late_ssem.at[int(across), j], late_rsem.at[j], device)

    def late_arrival(mine, jj):
        at, j = part(mine, jj), first_chunk(mine, jj)
        return remote(late_send.at[at], late_recv.at[at], late_ssem.at[0, j], late_rsem.at[j], beside)

    def takes(mine):
        return jnp.logical_or(odd, jnp.logical_and(inner, True if mine else source[1]))

    def gives(mine):
        return jnp.logical_or(side == 0, jnp.logical_and(inner, source[1] if mine else True))

    chunk_list = [(mine, jj) for mine in (False, True) for jj in range(parts)]
    ahead_list = [(mine, jj) for mine in (False, True) for jj in range(ahead_parts)]
    groups = [tuple(range(jj, min(jj + GROUP, parts))) for jj in range(0, parts, GROUP)]

    def weight(kind, h, level):
        return table_ref[kind, h, level].astype(F32) * factor(level)

    def token_weights(h, level):
        out = jnp.full((tokens, size), weight(0, h, level), F32)
        for kind in range(1, kinds):
            out = jnp.where(kind_col[...] == kind, weight(kind, h, level), out)
        return out

    def causal():
        row = lax.broadcasted_iota(jnp.int32, (tokens, tokens), 0)
        col = lax.broadcasted_iota(jnp.int32, (tokens, tokens), 1)
        return col <= row

    loads[0].wait()
    loads[1].wait()
    for index, (mine, jj) in enumerate(ahead_list):
        for h in chunk_heads(mine, jj, count=AHEAD):
            state = dot(k_ref[:, cols(h)], v_ref[:, cols(h)], TN)
            states[h] = state
            own_send[h] = state.astype(BF16)
        if index == 0:
            pl.semaphore_wait(barrier, greeted)

        @pl.when(gives(mine))
        def _():
            own_copy(mine, jj).start()

    for load in loads[2:]:
        load.wait()
    kind_col[...] = jnp.transpose(
        jnp.broadcast_to(kind_ref[...].astype(F32), (size, tokens))
    )

    def local_forward(mine, group):
        for h in chunk_heads(mine, *group):
            q = q_ref[:, cols(h)]
            scores = dot(q, k_ref[:, cols(h)], NT)
            attn = (jnp.where(causal(), scores, 0.0) * token_weights(h, 0)).astype(BF16)
            probs[h] = attn
            readout[h] = dot(attn, v_ref[:, cols(h)], NN)
            query_t[h] = jnp.transpose(q)

    def send_total(b, mine, jj):
        for h in chunk_heads(mine, jj, count=AHEAD):
            total_send[h] = states[h].astype(BF16)
        for t in reversed(range(1 << (b - 1))):
            total_copy(b, t, mine, jj).start()

    def add_level(b, mine, group):
        @pl.when(upper[b])
        def _():
            for h in chunk_heads(mine, *group):
                level = dot(q_ref[:, cols(h)], fwd_recv[b, h], NN)
                readout[h] += token_weights(h, b + 1) * level

    def add_state(b, mine, jj):
        for h in chunk_heads(mine, jj, count=AHEAD):
            states[h] += fwd_recv[b, h].astype(F32)

    def receive_first(mine, jj):
        @pl.when(takes(mine))
        def _():
            own_copy(mine, jj).wait_recv()
            add_state(0, mine, jj)

        if depth > 1:

            @pl.when(source[1])
            def _():
                send_total(1, mine, jj)

    def receive_total(b, mine, jj):
        @pl.when(upper[b])
        def _():
            total_copy(b, 0, mine, jj).wait_recv()
            if b > 1 and mine:
                relay_copy(b, mine, jj).start()

        if mine and b + 1 < depth:

            @pl.when(above[b])
            def _():
                add_state(b, mine, jj)

            @pl.when(source[b + 1])
            def _():
                send_total(b + 1, mine, jj)

    events = []
    stride = 3 * ahead_parts + 5
    everything = tuple(range(parts))
    for mine in (True, False):
        skip = 0 if mine else ahead_parts
        done = 2 * ahead_parts
        events += [
            (0.5 if mine else 1.5, local_forward, (mine, everything)),
            (1.4 + ahead_parts if mine else 1.5 + done, add_level, (0, mine, everything)),
        ]
        if depth > 1:
            events += [((1.6 if mine else 1.7) + done, add_level, (1, mine, everything))]
        for b in range(2, depth):
            now = 4.6 + 2 * (ahead_parts - 1) + (b - 2) * stride + (0 if mine else 1.4)
            events += [(now + 0.1, add_level, (b, mine, everything))]
        for jj in range(ahead_parts):
            events += [(1.0 + jj + skip, receive_first, (mine, jj))]
            if depth > 1:
                events += [(2.3 + jj + skip, receive_total, (1, mine, jj))]
            for b in range(2, depth):
                now = 4.6 + 2 * jj + (b - 2) * stride + (0 if mine else 1.4)
                events += [(now, receive_total, (b, mine, jj))]
    for _, event, at in sorted(events, key=lambda item: item[0]):
        event(*at)

    squares = jnp.zeros((tokens, size), F32)
    crosses = jnp.zeros((tokens, size), F32)
    for mine, jj in chunk_list:
        for h in chunk_heads(mine, jj):
            z = readout[h] * scale_ref[h]
            readout[h] = z
            squares += z * z
            crosses += gain_ref[:, cols(h)] * dy_ref[:, cols(h)].astype(F32) * z

    stat_send[0:1, :] = jnp.sum(jnp.transpose(squares), axis=0, keepdims=True)
    stat_send[1:2, :] = jnp.sum(jnp.transpose(crosses), axis=0, keepdims=True)
    stat_copies = [
        remote(
            stat_send, stat_recv.at[d - 1], stat_ssem.at[d - 1], stat_rsem.at[d - 1],
            {"head": lax.rem(me + d, head_count)},
        )
        for d in range(1, head_count)
    ]
    for copy in stat_copies:
        copy.start()
    square_row = stat_send[0:1, :]
    cross_row = stat_send[1:2, :]
    for d, copy in enumerate(stat_copies):
        copy.wait_recv()
        square_row += stat_recv[d, 0:1, :]
        cross_row += stat_recv[d, 1:2, :]
    features = width * head_count
    rms = jnp.sqrt(square_row / features + EPSILON)
    coef = cross_row / (features * rms * rms * rms)
    inv_col[...] = jnp.transpose(jnp.broadcast_to(1.0 / rms, (size, tokens)))
    coef_col[...] = jnp.transpose(jnp.broadcast_to(coef, (size, tokens)))

    def message(b, h, flag=1.0):
        total = None
        for kind in range(kinds):
            term = (weight(kind, h, b + 1) * flag) * kind_sums[h, :, pl.ds(kind * size, size)]
            total = term if total is None else total + term
        return total

    def send_bucket_grad(mine, jj):
        for h in chunk_heads(mine, jj):
            back_send[1, h] = message(1, h).astype(BF16)
        back_copy(1, mine, jj).start()

    for mine, group in [(mine, group) for mine in (False, True) for group in groups]:
        for h in chunk_heads(mine, *group):
            gain = gain_ref[:, cols(h)]
            z = readout[h]
            att_ref[:, cols(h)] = (z * inv_col[...] * gain).astype(BF16)
            grad = gain * dy_ref[:, cols(h)].astype(F32) * inv_col[...] - z * coef_col[...]
            grad = (grad * scale_ref[h]).astype(BF16)
            grad_out_ref[h] = grad
            masked = jnp.concatenate(
                [jnp.where(kind_col[...] == kind, grad.astype(F32), 0.0).astype(BF16) for kind in range(kinds)],
                axis=1,
            )
            kind_sums[h] = dot(query_t[h], masked, NN)
            grad_states[h] = jnp.zeros((size, size), F32)
        if not mine:
            for b in reversed(range(2, depth)):

                @pl.when(upper[b])
                def _():
                    for jj in group:
                        for h in chunk_heads(mine, jj):
                            half_send[b, h] = message(b, h).astype(BF16)
                        half_copy(b, mine, jj).start()

        if depth > 1:

            @pl.when(upper[1])
            def _():
                for jj in group:
                    send_bucket_grad(mine, jj)

    stores = [
        pltpu.make_async_copy(src, dst, store_sem.at[i])
        for i, (src, dst) in enumerate(
            ((att_ref, att_hbm), (gq_ref, gq_hbm), (gk_ref, gk_hbm), (gv_ref, gv_hbm))
        )
    ]
    stores[0].start()

    def local_backward(mine, group):
        for h in chunk_heads(mine, *group):
            grad = grad_out_ref[h]
            scores = dot(grad, v_ref[:, cols(h)], NT)
            dprobs = (jnp.where(causal(), scores, 0.0) * token_weights(h, 0)).astype(BF16)
            key_acc[h] = dot(dprobs, q_ref[:, cols(h)], TN)
            value_acc[h] = dot(probs[h], grad, TN)
            readout[h] = dot(dprobs, k_ref[:, cols(h)], NN)
        for b in range(depth):

            @pl.when(upper[b])
            def _():
                for h in chunk_heads(mine, *group):
                    level = dot(grad_out_ref[h], fwd_recv[b, h], NT)
                    readout[h] += token_weights(h, b + 1) * level

        for h in chunk_heads(mine, *group):
            gq_ref[:, cols(h)] = readout[h].astype(BF16)

    def pass_half(b, jj):
        @pl.when(upper[b])
        def _():
            half_copy(b, True, jj).wait_recv()
            for h in chunk_heads(True, jj):
                total = grad_states[h] + message(b, h) + half_recv[b, h].astype(F32)
                back_send[b, h] = total.astype(BF16)
            back_copy(b, True, jj).start()

    def gather_grads(b, mine, jj):
        @pl.when(source[b])
        def _():
            for t in range(1 << (b - 1)):
                back_arrival(t, mine, jj).wait_recv()
                for h in chunk_heads(mine, jj):
                    grad_states[h] += back_recv[t, h].astype(F32)

    def send_late(jj):
        @pl.when(late_gives)
        def _():
            for h in chunk_heads(True, jj):
                late_send[h] = grad_states[h].astype(BF16)
            for across in (True, False):
                late_copy(across, jj).start()

    def receive_late(mine, jj):
        @pl.when(late_takes)
        def _():
            late_arrival(mine, jj).wait_recv()
            for h in chunk_heads(mine, jj):
                grad_states[h] += late_recv[h].astype(F32)

    def send_last(mine, jj, when):
        @pl.when(jnp.logical_and(takes(mine), when))
        def _():
            flag = side.astype(F32)
            for h in chunk_heads(mine, jj):
                last_send[h] = (grad_states[h] + message(0, h, flag)).astype(BF16)
            last_copy(mine, jj).start()

    def finish(mine, jj):
        @pl.when(gives(mine))
        def _():
            last_copy(mine, jj).wait_recv()
            for h in chunk_heads(mine, jj):
                grad_states[h] += last_recv[h].astype(F32)

        for h in chunk_heads(mine, jj):
            state = grad_states[h].astype(BF16)
            gk_ref[:, cols(h)] = (key_acc[h] + dot(v_ref[:, cols(h)], state, NT)).astype(BF16)
            gv_ref[:, cols(h)] = (value_acc[h] + dot(k_ref[:, cols(h)], state, NN)).astype(BF16)

    def store_queries():
        stores[1].start()

    events = [(2.49, store_queries, ())]
    late = max(depth - 3, 0) * stride
    for group in groups:
        events += [
            (0.9 + 0.2 * group[0], local_backward, (False, group)),
            (2.3 + 0.2 * group[0], local_backward, (True, group)),
        ]
    for jj in range(parts):
        for b in range(2, depth):
            now = (depth - 1 - b) * stride
            events += [
                (now + 1.0 + jj, pass_half, (b, jj)),
                (now + 3.3 + 2 * jj, gather_grads, (b, True, jj)),
            ]
        if depth > 1:
            events += [
                (late + 2.5 + 0.01 * jj, gather_grads, (1, False, jj)),
                (late + 2.7 + 0.01 * jj, gather_grads, (1, True, jj)),
                (late + 3.4 + 2 * jj, send_late, (jj,)),
                (late + 3.5 + 2 * jj, send_last, (True, jj, late_gives)),
                (late + 5.0 + 2 * jj, receive_late, (True, jj)),
                (late + 5.2 + 2 * jj, receive_late, (False, jj)),
            ]
        events += [
            (late + 2.6 + 0.01 * jj, send_last, (False, jj, True)),
            (late + 2.8 + 0.01 * jj, send_last, (True, jj, jnp.logical_not(late_gives) if depth > 1 else True)),
            (late + 5.1 + 2 * jj, finish, (True, jj)),
            (late + 5.3 + 2 * jj, finish, (False, jj)),
        ]
    for _, event, at in sorted(events, key=lambda item: item[0]):
        event(*at)
    for store in stores[2:]:
        store.start()

    for copy in stat_copies:
        copy.wait_send()
    for mine, jj in ahead_list:

        @pl.when(gives(mine))
        def _():
            own_copy(mine, jj).wait_send()

        for b in range(1, depth):
            if mine or b == 1:

                @pl.when(source[b])
                def _():
                    for t in range(1 << (b - 1)):
                        total_copy(b, t, mine, jj).wait_send()

            if mine and b > 1:

                @pl.when(upper[b])
                def _():
                    relay_copy(b, mine, jj).wait_send()

    for mine, jj in chunk_list:
        if mine and depth > 1:

            @pl.when(late_gives)
            def _():
                for across in (True, False):
                    late_copy(across, jj).wait_send()

        @pl.when(takes(mine))
        def _():
            last_copy(mine, jj).wait_send()

        for b in range(1, depth):
            copy = back_copy if mine or b == 1 else half_copy

            @pl.when(upper[b])
            def _():
                copy(b, mine, jj).wait_send()

    for store in stores:
        store.wait()


def land(*refs):
    count = len(refs) // 2
    for source, target in zip(refs[:count], refs[count:]):
        target[...] = source[...]


def solution(mesh):
    ctx_count, head_count = mesh.shape["ctx"], mesh.shape["head"]
    depth = ctx_count.bit_length() - 1
    targets = max(ctx_count // 4, 1)

    def shards(queries, keys, values, grad_out, token_kind, level_table, head_scale, norm_gain):
        tokens, width = queries.shape
        kinds, heads, _ = level_table.shape
        size = width // heads
        chunks = heads // min(CHUNK, AHEAD)
        hbm = pl.BlockSpec(memory_space=pltpu.HBM)
        block = jax.ShapeDtypeStruct((tokens, width), BF16)
        square = (heads, size, size)
        dma = pltpu.SemaphoreType.DMA
        results = pl.pallas_call(
            functools.partial(kernel, ctx_count, head_count),
            out_shape=(block,) * 4,
            in_specs=[hbm] * 8,
            out_specs=(hbm,) * 4,
            scratch_shapes=[pltpu.VMEM((tokens, width), BF16)] * 4
            + [
                pltpu.VMEM((1, tokens), jnp.int32),
                pltpu.SMEM(level_table.shape, jnp.int32),
                pltpu.SMEM((heads,), F32),
                pltpu.VMEM((1, width), F32),
            ]
            + [pltpu.VMEM((tokens, width), BF16)] * 4
            + [pltpu.VMEM((tokens, size), F32)] * 3
            + [
                pltpu.VMEM(square, F32),
                pltpu.VMEM((heads, tokens, tokens), BF16),
                pltpu.VMEM((heads, size, tokens), BF16),
                pltpu.VMEM((heads, tokens, size), F32),
                pltpu.VMEM((heads, tokens, size), BF16),
                pltpu.VMEM((heads, size, kinds * size), F32),
                pltpu.VMEM(square, F32),
                pltpu.VMEM((heads, tokens, size), F32),
                pltpu.VMEM((heads, tokens, size), F32),
                pltpu.VMEM(square, BF16),
                pltpu.VMEM(square, BF16),
                pltpu.VMEM((depth,) + square, BF16),
                pltpu.VMEM((depth,) + square, BF16),
                pltpu.VMEM((depth,) + square, BF16),
                pltpu.VMEM((depth,) + square, BF16),
                pltpu.VMEM((targets,) + square, BF16),
                pltpu.VMEM(square, BF16),
                pltpu.VMEM(square, BF16),
                pltpu.VMEM(square, BF16),
                pltpu.VMEM(square, BF16),
                pltpu.VMEM((8, tokens), F32),
                pltpu.VMEM((head_count - 1, 8, tokens), F32),
                dma((8,)),
                dma((4,)),
                dma((chunks,)),
                dma((targets, chunks)),
                dma((depth, chunks)),
                dma((depth, chunks)),
                dma((depth, chunks)),
                dma((depth, chunks)),
                dma((depth, chunks)),
                dma((targets, chunks)),
                dma((chunks,)),
                dma((chunks,)),
                dma((2, chunks)),
                dma((chunks,)),
                dma((head_count - 1,)),
                dma((head_count - 1,)),
            ],
            compiler_params=pltpu.CompilerParams(
                collective_id=0, has_side_effects=True, vmem_limit_bytes=64 * 1024 * 1024
            ),
            cost_estimate=pl.CostEstimate(
                flops=36 * heads * tokens * size * size, bytes_accessed=16 * tokens * width, transcendentals=0
            ),
        )(
            queries, keys, values, grad_out,
            token_kind.reshape(1, tokens), level_table, head_scale, norm_gain.reshape(1, width),
        )
        rows = pl.BlockSpec((tokens // 2, width), lambda i: (i, 0))
        return pl.pallas_call(
            land,
            out_shape=(block,) * 4,
            grid=(2,),
            in_specs=[rows] * 4,
            out_specs=(rows,) * 4,
            compiler_params=pltpu.CompilerParams(vmem_limit_bytes=64 * 1024 * 1024),
        )(*results)

    in_specs = (
        P("ctx", "head"),
        P("ctx", "head"),
        P("ctx", "head"),
        P("ctx", "head"),
        P("ctx"),
        P(None, "head", None),
        P("head"),
        P("head"),
    )
    return jax.shard_map(
        shards, mesh=mesh, in_specs=in_specs, out_specs=(P("ctx", "head"),) * 4, check_vma=False
    )
```
